32 devices in a mesh: view: 4 (over y, x), band: 8 (over z, core).
Axes of the slice: x: 2, y: 2, z: 4, core: 2. Of those that a mesh axis runs over, the one named last changes fastest.
Arguments:
- features: float32 [4, 64, 512, 128], P('view', 'band'), may hold values from -6 to 6
- tempers: float32 [4, 64, 512], P('view', 'band'), may hold values from 0.5 to 80
- partners: int32 [4, 2], replicated, may hold values from 0 to 3, as said below
- conv_one: bfloat16 [3, 3, 128, 128], replicated, may hold values from -0.1875 to 0.1875
- conv_two: bfloat16 [3, 3, 128, 128], replicated, may hold values from -0.1875 to 0.1875
- query_weight: bfloat16 [128, 128], replicated, may hold values from -0.5 to 0.5
- key_weight: bfloat16 [128, 128], replicated, may hold values from -0.5 to 0.5
- value_weight: bfloat16 [128, 128], replicated, may hold values from -0.5 to 0.5
- out_weight: bfloat16 [128, 128], replicated, may hold values from -0.5 to 0.5
- norm_gain: float32 [128], replicated, may hold values from 0.25 to 1.75
- message_gain: float32 [128], replicated, may hold values from 0.25 to 1.75
Outputs:
- refined: float32 [4, 64, 512, 128], P('view', 'band')
The draws below stay inside these ranges and needn't reach their ends.
Inputs may be any that keep to these rules, and one draw needn't show every extreme that they name: Column 0 and column 1 are each a permutation of the 4 views; a view is never its own partner, and its two partners differ. At least one view has as its first partner the view 4 positions away from it (modulo 4).
All inputs are finite; a program needn't handle non-finite values.
Results may differ from the reference program's by a relative error of at most 0.0065.
Values may be sent and summed in bfloat16 or wider, within the bound.
No kernel may reach another device: no remote copies, remote signals or barrier semaphores. Data moves between devices by JAX's collectives and lax.ppermute only.
A program may use at most 64 MiB of HBM per device.

```python
import math
import jax
import jax.numpy as jnp
from jax import lax

FEATURES = 128
COLUMNS = 512
VIEWS = 4
HEIGHT = 64


def draw_tempers(key, part):
    level_key = jax.random.fold_in(jax.random.fold_in(key, 11), 0)
    shape = (VIEWS, HEIGHT, COLUMNS)
    levels = jnp.exp(jax.random.uniform(level_key, shape, jnp.float32, jnp.log(0.5), jnp.log(4.0)))
    return levels


def draw_partners(key, part):
    order_key, offset_key = jax.random.split(jax.random.fold_in(key, 23))
    ordering = jax.random.permutation(order_key, VIEWS).astype(jnp.int32)
    target = ((ordering[0] + VIEWS // 2) % VIEWS).astype(jnp.int32)
    found = jnp.argmax((ordering == target).astype(jnp.int32)).astype(jnp.int32)
    second_entry = ordering[1]
    ordering = ordering.at[1].set(target).at[found].set(second_entry)
    ordering = ordering.at[1].set(target)
    offset = jax.random.randint(offset_key, (), 2, VIEWS).astype(jnp.int32)
    positions = jnp.arange(VIEWS, dtype=jnp.int32)
    first_partner = jnp.zeros((VIEWS,), jnp.int32).at[ordering].set(ordering[(positions + 1) % VIEWS])
    second_partner = jnp.zeros((VIEWS,), jnp.int32).at[ordering].set(ordering[(positions + offset) % VIEWS])
    return jnp.stack([first_partner, second_partner], axis=1).astype(jnp.int32)


def block_levels(key, dims, pieces, low, high):
    level = 1.0
    for position, shards_of in pieces:
        draws = jax.random.uniform(jax.random.fold_in(jax.random.fold_in(key, 6), position), (shards_of,), jnp.float32, low / len(pieces), high / len(pieces))
        level = level * jnp.repeat(jnp.exp(draws), dims[position] // shards_of).reshape((-1,) + (1,) * (len(dims) - 1 - position))
    return level


def gaussian(stream_key, extent, scale, reach, shards=(), kind=jnp.bfloat16):
    drawn = jax.random.normal(stream_key, extent, jnp.float32) * scale
    if len(shards) > 0:
        drawn = block_levels(stream_key, extent, shards, -0.22, 0.18) * drawn
    return jnp.clip(drawn, min=-reach, max=reach).astype(kind)


def setup_inputs(seed: int = 0) -> dict:
    streams_of = jax.random.split(jax.random.key(seed), 12)
    features = gaussian(streams_of[0], (VIEWS, HEIGHT, COLUMNS, FEATURES), 1.0, 6.0, ((0, 4), (1, 8)), jnp.float32)
    tempers = draw_tempers(jax.random.fold_in(streams_of[11], 71), 0)
    partners = draw_partners(jax.random.fold_in(streams_of[11], 71), 0)
    conv_one = gaussian(streams_of[3], (3, 3, FEATURES, FEATURES), (9 * FEATURES) ** -0.5, 0.1875)
    conv_two = gaussian(streams_of[4], (3, 3, FEATURES, FEATURES), (9 * FEATURES) ** -0.5, 0.1875)
    query_weight = gaussian(streams_of[5], (FEATURES, FEATURES), FEATURES ** -0.5, 0.5)
    key_weight = gaussian(streams_of[6], (FEATURES, FEATURES), FEATURES ** -0.5, 0.5)
    value_weight = gaussian(streams_of[7], (FEATURES, FEATURES), FEATURES ** -0.5, 0.5)
    out_weight = gaussian(streams_of[8], (FEATURES, FEATURES), FEATURES ** -0.5, 0.5)
    norm_gain = jnp.clip(1.0 + 0.15 * jax.random.normal(streams_of[9], (FEATURES,), jnp.float32), 0.25, 1.75)
    message_gain = jnp.clip(1.0 + 0.15 * jax.random.normal(streams_of[10], (FEATURES,), jnp.float32), 0.25, 1.75)
    return dict(features=features, tempers=tempers, partners=partners, conv_one=conv_one, conv_two=conv_two, query_weight=query_weight, key_weight=key_weight, value_weight=value_weight, out_weight=out_weight, norm_gain=norm_gain, message_gain=message_gain)


epsilon = 1e-06

def root_norm(values, gain):
    mean_square = lax.optimization_barrier(jnp.mean(values * values, axis=-1, keepdims=True))
    return values * lax.rsqrt(mean_square + epsilon) * gain

def convolve(padded, kernel):
    leading = padded.shape[:-3]
    out_rows = padded.shape[-3] - 2
    columns = padded.shape[-2]
    channels = padded.shape[-1]
    widened = jnp.pad(padded, [(0, 0)] * len(leading) + [(0, 0), (1, 1), (0, 0)])
    summed = jnp.zeros(leading + (out_rows, columns, kernel.shape[-1]), jnp.float32)
    for row_tap in range(3):
        for col_tap in range(3):
            window = widened[..., row_tap:row_tap + out_rows, col_tap:col_tap + columns, :]
            product = jnp.dot(window.reshape(-1, channels), kernel[row_tap, col_tap], preferred_element_type=jnp.float32)
            summed = summed + product.reshape(summed.shape)
    return summed

def reference(features, tempers, partners, conv_one, conv_two, query_weight, key_weight, value_weight, out_weight, norm_gain, message_gain):
    row_pad = ((0, 0), (1, 1), (0, 0), (0, 0))
    first_input = jax.nn.silu(features).astype(jnp.bfloat16)
    state_one = features + convolve(jnp.pad(first_input, row_pad), conv_one)
    second_input = jax.nn.silu(state_one).astype(jnp.bfloat16)
    state_two = state_one + convolve(jnp.pad(second_input, row_pad), conv_two)
    normed = root_norm(state_two, norm_gain).astype(jnp.bfloat16)
    view_total, height, columns, channels = normed.shape
    flat_normed = normed.reshape(-1, channels)
    queries = jnp.dot(flat_normed, query_weight, preferred_element_type=jnp.float32).astype(jnp.bfloat16).reshape(normed.shape)
    key_all = jnp.dot(flat_normed, key_weight, preferred_element_type=jnp.float32).astype(jnp.bfloat16).reshape(normed.shape)
    value_all = jnp.dot(flat_normed, value_weight, preferred_element_type=jnp.float32).astype(jnp.bfloat16).reshape(normed.shape)
    key_pad = jnp.pad(key_all, row_pad)
    value_pad = jnp.pad(value_all, row_pad)
    factor = 1.0 / math.sqrt(channels)
    zero_index = jnp.zeros((), jnp.int32)

    def attend(flat_index):
        view_index = (flat_index // height).astype(jnp.int32)
        row_index = (flat_index % height).astype(jnp.int32)
        query_row = queries[view_index, row_index]
        temper_row = tempers[view_index, row_index] * factor
        summed = jnp.zeros((columns, channels), jnp.float32)
        for partner in range(2):
            source = partners[view_index, partner].astype(jnp.int32)
            starts = (source, row_index, zero_index, zero_index)
            key_rows = lax.dynamic_slice(key_pad, starts, (1, 3, columns, channels)).reshape(3 * columns, channels)
            value_rows = lax.dynamic_slice(value_pad, starts, (1, 3, columns, channels)).reshape(3 * columns, channels)
            scores = jnp.dot(query_row, key_rows.T, preferred_element_type=jnp.float32) * temper_row[:, None]
            row_peak = lax.optimization_barrier(jnp.max(scores, axis=-1, keepdims=True))
            lifted = jnp.exp(scores - row_peak)
            shares = (lifted / lax.optimization_barrier(jnp.sum(lifted, axis=-1, keepdims=True))).astype(jnp.bfloat16)
            blended = jnp.dot(shares, value_rows, preferred_element_type=jnp.float32).astype(jnp.bfloat16)
            summed = summed + jnp.dot(blended, out_weight, preferred_element_type=jnp.float32)
        return summed
    messages = lax.map(attend, jnp.arange(view_total * height, dtype=jnp.int32)).reshape(state_two.shape)
    return state_two + root_norm(messages, message_gain)
```

```python
import functools
import math

import jax
import jax.numpy as jnp
from jax import lax
from jax.experimental import pallas as pl
from jax.experimental.pallas import tpu as pltpu
from jax.sharding import PartitionSpec as P

epsilon = 1e-06
vmem_bytes = 56 * 1024 * 1024


def pair_weights(kernel):
    taps, _, channels, out_channels = kernel.shape
    zero = jnp.zeros_like(kernel[:1])
    first = jnp.concatenate([kernel, zero], axis=0)
    second = jnp.concatenate([zero, kernel], axis=0)
    both = jnp.stack([first, second], axis=3)
    return both.reshape((taps + 1) * taps * channels, 2 * out_channels)


def silu(v):
    return v / (1.0 + jnp.exp(-v))


def spread(value, pad, out):
    columns = value.shape[0]
    pad[8 : 8 + columns] = value
    left = pad[7 : 7 + columns]
    right = pad[9 : 9 + columns]
    out[...] = jnp.concatenate([left, value, right], axis=-1).astype(jnp.bfloat16)


def row_pair(x_ref, first, weights):
    lhs = jnp.concatenate([x_ref[first + j] for j in range(4)], axis=-1)
    return jnp.dot(lhs, weights[...], preferred_element_type=jnp.float32)


def residual_body(
    flags, cells, above, below, weights_one, weights_two, gain, tempers, mixing,
    state_out, edge_out, middle_out, query_out, pad, x_one, x_two, state_one,
):
    rows, columns, channels = cells.shape
    zeros = jnp.zeros((8, channels), jnp.float32)
    for slot in range(2):
        pad[slot, 0:8] = zeros
        pad[slot, 8 + columns : 16 + columns] = zeros
    for r in range(rows + 4):
        if r < 2:
            value = above[r].astype(jnp.float32)
        elif r < rows + 2:
            value = cells[r - 2]
        else:
            value = below[r - rows - 2].astype(jnp.float32)
        spread(silu(value), pad.at[r % 2], x_one.at[r])
    for first in range(0, rows + 2, 2):
        out = row_pair(x_one, first, weights_one)
        for o in range(2):
            r = first + o
            if r == 0:
                state = above[1].astype(jnp.float32) + out[:, :channels]
            elif r == rows + 1:
                state = below[0].astype(jnp.float32) + out[:, channels:]
            else:
                state = cells[r - 1] + out[:, o * channels : (o + 1) * channels]
                state_one[r - 1] = state
            lifted = silu(state)
            if r == 0:
                lifted = jnp.where(flags[0] > 0, lifted, 0.0)
            elif r == rows + 1:
                lifted = jnp.where(flags[1] > 0, lifted, 0.0)
            spread(lifted, pad.at[o], x_two.at[r])
    quarter = rows // 4
    for first in range(0, rows, 2):
        out = row_pair(x_two, first, weights_two)
        for o in range(2):
            r = first + o
            state = state_one[r] + out[:, o * channels : (o + 1) * channels]
            state_out[r] = state
            scale = lax.rsqrt(jnp.mean(state * state, axis=-1, keepdims=True) + epsilon)
            normed = (state * scale * gain[...]).astype(jnp.bfloat16)
            if r < quarter:
                edge_out[r] = normed
            elif r >= rows - quarter:
                edge_out[r - rows + 2 * quarter] = normed
            else:
                middle_out[r - quarter] = normed
            query = jnp.dot(normed, mixing[...], preferred_element_type=jnp.float32)
            query_out[r] = (query * tempers[:, r : r + 1]).astype(jnp.bfloat16)


def residual_step(flags, cells, above, below, weights_one, weights_two, gain, tempers, mixing):
    rows, columns, channels = cells.shape
    whole = pl.BlockSpec(memory_space=pltpu.VMEM)
    half = rows // 4 * 2
    return pl.pallas_call(
        residual_body,
        in_specs=[pl.BlockSpec(memory_space=pltpu.SMEM)] + [whole] * 8,
        out_specs=[whole] * 4,
        out_shape=[
            jax.ShapeDtypeStruct(cells.shape, jnp.float32),
            jax.ShapeDtypeStruct((half, columns, channels), jnp.bfloat16),
            jax.ShapeDtypeStruct((rows - half, columns, channels), jnp.bfloat16),
            jax.ShapeDtypeStruct(cells.shape, jnp.bfloat16),
        ],
        scratch_shapes=[
            pltpu.VMEM((2, columns + 16, channels), jnp.float32),
            pltpu.VMEM((rows + 4, columns, 3 * channels), jnp.bfloat16),
            pltpu.VMEM((rows + 2, columns, 3 * channels), jnp.bfloat16),
            pltpu.VMEM(cells.shape, jnp.float32),
        ],
        compiler_params=pltpu.CompilerParams(vmem_limit_bytes=vmem_bytes),
        name="residual_convolutions",
    )(flags, cells, above, below, weights_one, weights_two, gain, tempers, mixing)


def blend(query, window, store):
    keys, channels = window.shape
    extended = jnp.concatenate([window, jnp.ones((keys, channels), jnp.bfloat16)], axis=1)
    columns = query.shape[0]
    block = 128 if columns % 128 == 0 else columns
    for start in range(0, columns, block):
        scores = lax.dot_general(
            query[start : start + block],
            window,
            (((1,), (1,)), ((), ())),
            preferred_element_type=jnp.float32,
        )
        peak = jnp.max(scores, axis=-1, keepdims=True)
        lifted = jnp.exp2(scores - peak).astype(jnp.bfloat16)
        total = jnp.dot(lifted, extended, preferred_element_type=jnp.float32)
        store(start, block, total[:, :channels] / total[:, channels:])


def attend_near_body(query, keys, out):
    row = pl.program_id(0)
    columns, channels = query.shape[1:]
    window = keys[pl.ds(row, 3)].reshape(3 * columns, channels)

    def store(start, block, value):
        out[0, start : start + block] = value

    blend(query[0], window, store)


def attend_far_body(query, keys, near, state, value_out, gain, out):
    row = pl.program_id(0)
    columns, channels = query.shape[1:]
    window = keys[pl.ds(row, 3)].reshape(3 * columns, channels)

    def store(start, block, value):
        both = (value + near[0, start : start + block]).astype(jnp.bfloat16)
        message = jnp.dot(both, value_out[...], preferred_element_type=jnp.float32)
        scale = lax.rsqrt(jnp.mean(message * message, axis=-1, keepdims=True) + epsilon)
        out[0, start : start + block] = state[0, start : start + block] + message * scale * gain[...]

    blend(query[0], window, store)


def attend(body, name, query, keys, *rest):
    rows, columns, channels = query.shape
    row_spec = pl.BlockSpec((1, columns, channels), lambda i: (i, 0, 0))
    whole = pl.BlockSpec(memory_space=pltpu.VMEM)
    rest_specs = [row_spec if a.ndim == 3 else whole for a in rest]
    return pl.pallas_call(
        body,
        grid=(rows,),
        in_specs=[row_spec, whole] + rest_specs,
        out_specs=row_spec,
        out_shape=jax.ShapeDtypeStruct(query.shape, jnp.float32),
        compiler_params=pltpu.CompilerParams(vmem_limit_bytes=vmem_bytes),
        name=name,
    )(query, keys, *rest)


def swap(cells, views, offset):
    return lax.ppermute(cells, "view", [(i, i ^ offset) for i in range(views)])


def gather_views(cells, views):
    half = cells.shape[0] // 2
    held = {}
    for offset in range(1, views):
        low = offset & -offset
        high = 1 << (offset.bit_length() - 1)
        if low == high:
            held[offset] = swap(cells, views, offset)
        else:
            first = swap(held[offset ^ low][:half], views, low)
            second = swap(held[offset ^ high][half:], views, high)
            held[offset] = jnp.concatenate([first, second], axis=0)
    return held


def choose(held, offset, low, high):
    picked = held[low]
    for candidate in range(low + 1, high + 1):
        picked = jnp.where(offset == candidate, held[candidate], picked)
    return picked


def per_device(
    features, tempers, partners, conv_one, conv_two, query_weight, key_weight,
    value_weight, out_weight, norm_gain, message_gain,
):
    views = lax.axis_size("view")
    bands = lax.axis_size("band")
    band = lax.axis_index("band")
    view = lax.axis_index("view")
    cells = features[0]
    rows, columns, channels = cells.shape
    upward = [(i + 1, i) for i in range(bands - 1)]
    downward = [(i, i + 1) for i in range(bands - 1)]

    above = lax.ppermute(cells[rows - 2 :].astype(jnp.bfloat16), "band", downward)
    below = lax.ppermute(cells[:2].astype(jnp.bfloat16), "band", upward)
    flags = jnp.stack([band > 0, band < bands - 1]).astype(jnp.int32)
    factor = math.log2(math.e) / math.sqrt(channels)
    columns_tempers = tempers[0].T * factor
    mixing = lax.dot_general(
        query_weight, key_weight, (((1,), (1,)), ((), ())), preferred_element_type=jnp.float32
    ).astype(jnp.bfloat16)
    value_out = jnp.dot(value_weight, out_weight, preferred_element_type=jnp.float32).astype(
        jnp.bfloat16
    )
    state_two, edge, middle, queries = residual_step(
        flags, cells, above, below, pair_weights(conv_one), pair_weights(conv_two),
        norm_gain[None], columns_tempers, mixing,
    )
    edges = gather_views(edge, views)
    middles = gather_views(middle, views)

    offsets = jnp.bitwise_xor(lax.dynamic_index_in_dim(partners, view, 0, keepdims=False), view)
    near, far = jnp.min(offsets), jnp.max(offsets)
    bounds = ((near, 1, max(1, views - 2)), (far, min(2, views - 1), views - 1))
    half = edge.shape[0] // 2
    picked_edges = [choose(edges, *bound) for bound in bounds]
    picked_middles = [choose(middles, *bound) for bound in bounds]
    heads = jnp.stack([e[:1] for e in picked_edges])
    tails = jnp.stack([e[-1:] for e in picked_edges])
    from_above = lax.ppermute(tails, "band", downward)
    from_below = lax.ppermute(heads, "band", upward)
    keys = [
        jnp.concatenate(
            [from_above[i], picked_edges[i][:half], picked_middles[i], picked_edges[i][half:],
             from_below[i]], axis=0,
        )
        for i in range(2)
    ]
    near_blend = attend(attend_near_body, "attend_near", queries, keys[0])
    refined = attend(
        attend_far_body, "attend_far", queries, keys[1], near_blend, state_two, value_out,
        message_gain[None],
    )
    return refined[None]


def solution(mesh):
    whole = P()
    in_specs = (P("view", "band", None, None), P("view", "band", None)) + (whole,) * 9
    return jax.shard_map(
        per_device, mesh=mesh, in_specs=in_specs,
        out_specs=P("view", "band", None, None), check_vma=False,
    )
```

```python
import functools
import math

import jax
import jax.numpy as jnp
from jax import lax
from jax.experimental import pallas as pl
from jax.experimental.pallas import tpu as pltpu
from jax.sharding import PartitionSpec as P

epsilon = 1e-06
vmem_bytes = 28 * 1024 * 1024
whole_vmem_bytes = 56 * 1024 * 1024
in_vmem = pl.BlockSpec(memory_space=pltpu.VMEM)
in_smem = pl.BlockSpec(memory_space=pltpu.SMEM)
anywhere = pl.BlockSpec(memory_space=pl.ANY)


def silu(v):
    half = 0.5 * v
    return half * jnp.tanh(half) + half


def scaled(values, gain):
    channels = values.shape[-1]
    squares = (values * values).astype(jnp.bfloat16)
    ones = jnp.ones((channels, channels), jnp.bfloat16)
    mean_square = jnp.dot(squares, ones, preferred_element_type=jnp.float32) * (1.0 / channels)
    return values * lax.rsqrt(mean_square + epsilon) * gain


class Copies:
    def __init__(self, semaphores):
        self.semaphores = semaphores
        self.count = 0

    def start(self, source, target):
        copy = pltpu.make_async_copy(source, target, self.semaphores.at[self.count])
        self.count += 1
        copy.start()
        return copy

    def start_one(self, sources, chosen, target):
        slot = self.semaphores.at[self.count]
        self.count += 1
        for i, source in enumerate(sources):

            @pl.when(chosen == i)
            def _(source=source):
                pltpu.make_async_copy(source, target, slot).start()

        return pltpu.make_async_copy(sources[0], target, slot)


def clear(pad):
    slots, length, channels = pad.shape
    zeros = jnp.zeros((8, channels), jnp.float32)
    for slot in range(slots):
        pad[slot, 0:8] = zeros
        pad[slot, length - 8 : length] = zeros


def place(value, pad, slot):
    pad[slot, 8 : 8 + value.shape[0]] = value


def pack(kernel, out):
    channels = kernel.shape[2]
    zero = jnp.zeros((channels, channels), jnp.bfloat16)
    for j in range(4):
        for b in range(3):
            rows = pl.ds((3 * j + b) * channels, channels)
            out[rows, :channels] = kernel[j, b] if j < 3 else zero
            out[rows, channels:] = kernel[j - 1, b] if j > 0 else zero


def row_pair(pad, first, weights):
    columns = pad.shape[1] - 16
    lhs = [pad[first + j, 7 + b : 7 + b + columns] for j in range(4) for b in range(3)]
    lhs = jnp.concatenate(lhs, axis=-1).astype(jnp.bfloat16)
    return jnp.dot(lhs, weights[...], preferred_element_type=jnp.float32)


def ask(norm, slots, query_weight, key_weight, tempers, rows_of, query):
    channels = norm.shape[-1]
    mixing = lax.dot_general(
        query_weight[...],
        key_weight[...],
        (((1,), (1,)), ((), ())),
        preferred_element_type=jnp.float32,
    ).astype(jnp.bfloat16)
    scales = tempers[...].T * (math.log2(math.e) / math.sqrt(channels))
    for slot in range(slots):
        mixed = jnp.dot(norm[slot], mixing, preferred_element_type=jnp.float32)
        r = rows_of(slot)
        query[slot] = (mixed * scales[:, r : r + 1]).astype(jnp.bfloat16)


def middle_body(
    cells, one, two, query_weight, key_weight, tempers, gain,
    state_one_out, state_out, norm_out, query_out,
    held, one_held, two_held, query_held, key_held, tempers_held, gain_held,
    w1, w2, state_one, state_two, norm, query, x1, x2, sems,
):
    rows = cells.shape[0]
    channels = cells.shape[2]
    copies = Copies(sems)
    loads = [copies.start(cells.at[r], held.at[r]) for r in range(4)]
    later = [copies.start(one, one_held)]
    later += [copies.start(cells.at[r], held.at[r]) for r in range(4, rows)]
    later += [
        copies.start(two, two_held),
        copies.start(gain, gain_held),
        copies.start(query_weight, query_held),
        copies.start(key_weight, key_held),
        copies.start(tempers, tempers_held),
    ]
    clear(x1)
    clear(x2)

    def convolve_one(first):
        out = row_pair(x1, first, w1)
        for o in range(2):
            r = first + 1 + o
            state = held[r] + out[:, o * channels : (o + 1) * channels]
            state_one[r - 1] = state
            place(silu(state), x2, r - 1)

    def convolve_two(first):
        out = row_pair(x2, first, w2)
        for o in range(2):
            slot = first + o
            state = state_one[slot + 1] + out[:, o * channels : (o + 1) * channels]
            state_two[slot] = state
            norm[slot] = scaled(state, gain_held[...]).astype(jnp.bfloat16)

    for load in loads:
        load.wait()
    for r in range(4):
        place(silu(held[r]), x1, r)
    for load in later:
        load.wait()
    pack(one_held, w1)
    pack(two_held, w2)
    for first in range(0, rows - 2, 2):
        convolve_one(first)
        for r in range(first + 4, min(first + 6, rows)):
            place(silu(held[r]), x1, r)
        if first >= 2:
            convolve_two(first - 2)
    stores = [
        copies.start(norm, norm_out),
        copies.start(state_one.at[pl.ds(0, 2)], state_one_out.at[pl.ds(0, 2)]),
        copies.start(state_one.at[pl.ds(rows - 4, 2)], state_one_out.at[pl.ds(2, 2)]),
        copies.start(state_two, state_out),
    ]
    ask(norm, rows - 4, query_held, key_held, tempers_held, lambda slot: slot + 2, query)
    stores.append(copies.start(query, query_out))
    for store in stores:
        store.wait()


def scratch(*arrays):
    return [pltpu.VMEM(shape, kind) for shape, kind in arrays]


def middle_rows(cells, one, two, query_weight, key_weight, tempers, gain):
    rows, columns, channels = cells.shape
    row = (columns, channels)
    padded = (columns + 16, channels)
    packed = ((12 * channels, 2 * channels), jnp.bfloat16)
    operands = (cells, one, two, query_weight, key_weight, tempers, gain)
    return pl.pallas_call(
        middle_body,
        in_specs=[anywhere] * 7,
        out_specs=[anywhere] * 4,
        out_shape=[
            jax.ShapeDtypeStruct((4, *row), jnp.float32),
            jax.ShapeDtypeStruct((rows - 4, *row), jnp.float32),
            jax.ShapeDtypeStruct((rows - 4, *row), jnp.bfloat16),
            jax.ShapeDtypeStruct((rows - 4, *row), jnp.bfloat16),
        ],
        scratch_shapes=[
            *scratch(*[(a.shape, a.dtype) for a in operands]),
            *scratch(
                packed,
                packed,
                ((rows - 2, *row), jnp.float32),
                ((rows - 4, *row), jnp.float32),
                ((rows - 4, *row), jnp.bfloat16),
                ((rows - 4, *row), jnp.bfloat16),
                ((rows, *padded), jnp.float32),
                ((rows - 2, *padded), jnp.float32),
            ),
            pltpu.SemaphoreType.DMA((rows + 11,)),
        ],
        compiler_params=pltpu.CompilerParams(vmem_limit_bytes=whole_vmem_bytes),
        name="residual_middle",
    )(*operands)


def edge_body(
    cells, mate, cross, one, two, state_one, query_weight, key_weight, tempers, gain,
    state_out, norm_out, query_out,
    held, mate_held, cross_held, one_held, two_held, state_held, query_held, key_held,
    tempers_held, gain_held, w1, w2, state_two, norm, query, x1, x2, sems,
):
    rows = cells.shape[0]
    channels = cells.shape[2]
    first_band, last_band, odd = band_place()
    copies = Copies(sems)
    loads = [
        copies.start(cells.at[pl.ds(0, 2)], held.at[pl.ds(0, 2)]),
        copies.start(cells.at[pl.ds(rows - 2, 2)], held.at[pl.ds(2, 2)]),
        copies.start(mate, mate_held),
        copies.start(cross, cross_held),
    ]
    later = [
        copies.start(one, one_held),
        copies.start(two, two_held),
        copies.start(state_one, state_held),
        copies.start(query_weight, query_held),
        copies.start(key_weight, key_held),
        copies.start(tempers, tempers_held),
        copies.start(gain, gain_held),
    ]
    clear(x1)
    clear(x2)
    for load in loads:
        load.wait()
    for r in range(2):
        place(silu(held[r]), x1, 2 + r)
        place(silu(held[2 + r]), x1, 4 + r)
    outside = []
    for r in range(2):
        mate_row = mate_held[r].astype(jnp.float32)
        cross_row = cross_held[r].astype(jnp.float32)
        over = jnp.where(first_band, 0.0, jnp.where(odd, mate_row, cross_row))
        under = jnp.where(last_band, 0.0, jnp.where(odd, cross_row, mate_row))
        place(silu(over), x1, r)
        place(silu(under), x1, 6 + r)
        outside.append((over, under))
    over, under = outside[1][0], outside[0][1]
    for load in later:
        load.wait()
    pack(one_held, w1)
    pack(two_held, w2)
    out = row_pair(x1, 0, w1)
    over = over + out[:, :channels]
    top = held[0] + out[:, channels:]
    out = row_pair(x1, 4, w1)
    bottom = held[3] + out[:, :channels]
    under = under + out[:, channels:]
    for r in range(2):
        place(silu(state_held[r]), x2, 2 + r)
        place(silu(state_held[2 + r]), x2, 4 + r)
    place(jnp.where(first_band, 0.0, silu(over)), x2, 0)
    place(silu(top), x2, 1)
    place(silu(bottom), x2, 6)
    place(jnp.where(last_band, 0.0, silu(under)), x2, 7)
    for slot, states in ((0, (top, state_held[0])), (2, (state_held[3], bottom))):
        out = row_pair(x2, 2 * slot, w2)
        for o in range(2):
            state = states[o] + out[:, o * channels : (o + 1) * channels]
            state_two[slot + o] = state
            norm[slot + o] = scaled(state, gain_held[...]).astype(jnp.bfloat16)
    stores = [copies.start(norm, norm_out), copies.start(state_two, state_out)]
    ask(
        norm, 4, query_held, key_held, tempers_held,
        lambda slot: slot if slot < 2 else rows - 4 + slot, query,
    )
    stores.append(copies.start(query, query_out))
    for store in stores:
        store.wait()


def edge_rows(cells, mate, cross, one, two, state_one, query_weight, key_weight, tempers, gain):
    columns, channels = cells.shape[1:]
    row = (columns, channels)
    padded = (columns + 16, channels)
    packed = ((12 * channels, 2 * channels), jnp.bfloat16)
    operands = (
        cells, mate, cross, one, two, state_one, query_weight, key_weight, tempers, gain
    )
    return pl.pallas_call(
        edge_body,
        in_specs=[anywhere] * 10,
        out_specs=[anywhere] * 3,
        out_shape=[
            jax.ShapeDtypeStruct((4, *row), jnp.float32),
            jax.ShapeDtypeStruct((4, *row), jnp.bfloat16),
            jax.ShapeDtypeStruct((4, *row), jnp.bfloat16),
        ],
        scratch_shapes=[
            *scratch(((4, *row), jnp.float32), *[(a.shape, a.dtype) for a in operands[1:]]),
            *scratch(
                packed,
                packed,
                ((4, *row), jnp.float32),
                ((4, *row), jnp.bfloat16),
                ((4, *row), jnp.bfloat16),
                ((8, *padded), jnp.float32),
                ((8, *padded), jnp.float32),
            ),
            pltpu.SemaphoreType.DMA((14,)),
        ],
        compiler_params=pltpu.CompilerParams(vmem_limit_bytes=whole_vmem_bytes),
        name="residual_edge",
    )(*operands)


def band_place():
    band = lax.axis_index("band")
    return band == 0, band == lax.axis_size("band") - 1, lax.rem(band, 2) == 1


def blend(query, window, store):
    keys, channels = window.shape
    extended = jnp.concatenate([window, jnp.ones((keys, channels), jnp.bfloat16)], axis=1)
    columns = query.shape[0]
    block = 128 if columns % 128 == 0 else columns
    for start in range(0, columns, block):
        scores = lax.dot_general(
            query[pl.ds(start, block)],
            window,
            (((1,), (1,)), ((), ())),
            preferred_element_type=jnp.float32,
        )
        peak = jnp.max(scores, axis=-1, keepdims=True)
        lifted = jnp.exp2(scores - peak).astype(jnp.bfloat16)
        total = jnp.dot(lifted, extended, preferred_element_type=jnp.float32)
        store(pl.ds(start, block), total[:, :channels] / total[:, channels:])


def pick(chosen, candidates):
    picked = candidates[0]
    for i, candidate in enumerate(candidates[1:], 1):
        picked = jnp.where(chosen == i, candidate, picked)
    return picked


def gather_keys(chosen, edges, middles, mate, cross, keys):
    rows = keys.shape[0] - 2
    first_band, last_band, odd = band_place()
    above = jnp.where(odd, mate[0], cross[0])
    below = jnp.where(odd, cross[0], mate[0])
    keys[0] = jnp.where(first_band, jnp.zeros_like(above), above)
    keys[rows + 1] = jnp.where(last_band, jnp.zeros_like(below), below)
    for r in range(2):
        keys[1 + r] = pick(chosen, [edge[r] for edge in edges])
        keys[rows - 1 + r] = pick(chosen, [edge[2 + r] for edge in edges])
    for r in range(rows - 4):
        keys[3 + r] = pick(chosen, [middle[r] for middle in middles])


def band_row(edge, middle, r):
    inner = middle.shape[0]
    if r < 2:
        return edge.at[r]
    if r < inner + 2:
        return middle.at[r - 2]
    return edge.at[r - inner]


def attend_near_body(count, chosen, *refs):
    edges, middles = refs[:count], refs[count : 2 * count]
    mate, cross, query_edge, query_middle, out, keys = refs[2 * count :]
    rows, columns, channels = out.shape
    gather_keys(chosen[0], edges, middles, mate, cross, keys)
    for r in range(rows):
        window = keys[r : r + 3].reshape(3 * columns, channels)

        def store(place, value, r=r):
            out[r, place] = value.astype(jnp.bfloat16)

        blend(band_row(query_edge, query_middle, r), window, store)


def attend_far_body(count, chosen, *refs):
    edges, middles = refs[:count], refs[count : 2 * count]
    (
        mate, cross, query_edge, query_middle, near, state_edge, state_middle, value_out, gain,
        out, keys, both,
    ) = refs[2 * count :]
    rows, columns, channels = out.shape
    gather_keys(chosen[0], edges, middles, mate, cross, keys)
    for r in range(rows):
        window = keys[r : r + 3].reshape(3 * columns, channels)

        def store(place, value, r=r):
            both[r, place] = (value + near[r, place].astype(jnp.float32)).astype(jnp.bfloat16)

        blend(band_row(query_edge, query_middle, r), window, store)
    for r in range(rows):
        message = jnp.dot(both[r], value_out[...], preferred_element_type=jnp.float32)
        state = band_row(state_edge, state_middle, r)[...]
        out[r] = state + scaled(message, gain[...])


def attend(body, name, chosen, edges, middles, mate, cross, queries, rest, out_type, extra):
    query_edge, query_middle = queries
    rows = query_edge.shape[0] + query_middle.shape[0]
    columns, channels = query_edge.shape[1:]
    operands = [*edges, *middles, mate, cross, *queries, *rest]
    return pl.pallas_call(
        functools.partial(body, len(edges)),
        in_specs=[in_smem] + [in_vmem] * len(operands),
        out_specs=in_vmem,
        out_shape=jax.ShapeDtypeStruct((rows, columns, channels), out_type),
        scratch_shapes=[
            pltpu.VMEM((rows + 2, columns, channels), jnp.bfloat16),
            *[pltpu.VMEM((rows, columns, channels), kind) for kind in extra],
        ],
        compiler_params=pltpu.CompilerParams(vmem_limit_bytes=vmem_bytes),
        name=name,
    )(chosen, *operands)


def swap(cells, views, offset):
    return lax.ppermute(cells, "view", [(i, i ^ offset) for i in range(views)])


def gather_direct(cells, views):
    return {1 << i: swap(cells, views, 1 << i) for i in range((views - 1).bit_length())}


def gather_relayed(edges, middles, views):
    for offset in range(1, views):
        low = offset & -offset
        high = 1 << (offset.bit_length() - 1)
        if low != high:
            edges[offset] = swap(edges[offset ^ high], views, high)
            middles[offset] = swap(middles[offset ^ low], views, low)


def swap_bands(head, tail, odd, bands):
    mates = [(i, i ^ 1) for i in range(bands)]
    crosses = [(i, i + 1) for i in range(1, bands - 1, 2)]
    crosses = crosses + [(j, i) for i, j in crosses]
    mate = lax.ppermute(jnp.where(odd, head, tail), "band", mates)
    cross = lax.ppermute(jnp.where(odd, tail, head), "band", crosses)
    return mate, cross


def per_device(
    features, tempers, partners, conv_one, conv_two, query_weight, key_weight,
    value_weight, out_weight, norm_gain, message_gain,
):
    views = lax.axis_size("view")
    bands = lax.axis_size("band")
    odd = lax.axis_index("band") % 2 > 0
    view = lax.axis_index("view")
    cells, temper, gain = features[0], tempers[0], norm_gain[None]
    rows = cells.shape[0]

    state_one, state_middle, middle, query_middle = middle_rows(
        cells, conv_one, conv_two, query_weight, key_weight, temper, gain
    )
    middles = gather_direct(middle, views)
    head, tail = cells[:2].astype(jnp.bfloat16), cells[rows - 2 :].astype(jnp.bfloat16)
    mate, cross = swap_bands(head, tail, odd, bands)
    state_edge, edge, query_edge = edge_rows(
        cells, mate, cross, conv_one, conv_two, state_one, query_weight, key_weight, temper, gain
    )
    queries = (query_edge, query_middle)
    edges = gather_direct(edge, views)
    edges, middles = lax.optimization_barrier((edges, middles))
    gather_relayed(edges, middles, views)
    value_out = jnp.dot(value_weight, out_weight, preferred_element_type=jnp.float32).astype(
        jnp.bfloat16
    )

    offsets = jnp.bitwise_xor(lax.dynamic_index_in_dim(partners, view, 0, keepdims=False), view)

    def keys_of(offset, low, high, after=None):
        chosen = offset - low
        some_edges = [edges[i] for i in range(low, high + 1)]
        some_middles = [middles[i] for i in range(low, high + 1)]
        if after is not None:
            some_edges, some_middles, after = lax.optimization_barrier(
                (some_edges, some_middles, after)
            )
        tail = pick(chosen, [e[-1:] for e in some_edges])
        head = pick(chosen, [e[:1] for e in some_edges])
        halos = swap_bands(head, tail, odd, bands)
        return chosen[None], some_edges, some_middles, *halos

    near_keys = keys_of(jnp.min(offsets), 1, max(1, views - 2))
    near_blend = attend(
        attend_near_body, "attend_near", *near_keys, queries, (), jnp.bfloat16, []
    )
    far_keys = keys_of(jnp.max(offsets), min(2, views - 1), views - 1, near_blend)
    refined = attend(
        attend_far_body, "attend_far", *far_keys, queries,
        (near_blend, state_edge, state_middle, value_out, message_gain[None]), jnp.float32,
        [jnp.bfloat16],
    )
    return refined[None]


def solution(mesh):
    whole = P()
    in_specs = (P("view", "band", None, None), P("view", "band", None)) + (whole,) * 9
    return jax.shard_map(
        per_device, mesh=mesh, in_specs=in_specs,
        out_specs=P("view", "band", None, None), check_vma=False,
    )
```

```python
import functools
import math

import jax
import jax.numpy as jnp
from jax import lax
from jax.experimental import pallas as pl
from jax.experimental.pallas import tpu as pltpu
from jax.sharding import PartitionSpec as P

epsilon = 1e-06
vmem_bytes = 28 * 1024 * 1024
near_vmem_bytes = 44 * 1024 * 1024
whole_vmem_bytes = 56 * 1024 * 1024
in_vmem = pl.BlockSpec(memory_space=pltpu.VMEM)
in_smem = pl.BlockSpec(memory_space=pltpu.SMEM)
no_cost = pl.CostEstimate(flops=0, bytes_accessed=0, transcendentals=0)
anywhere = pl.BlockSpec(memory_space=pl.ANY)


def silu(v):
    half = 0.5 * v
    return half * jnp.tanh(half) + half


def scaled(values, gain):
    channels = values.shape[-1]
    squares = (values * values).astype(jnp.bfloat16)
    ones = jnp.ones((channels, channels), jnp.bfloat16)
    mean_square = jnp.dot(squares, ones, preferred_element_type=jnp.float32) * (1.0 / channels)
    return values * lax.rsqrt(mean_square + epsilon) * gain


class Copies:
    def __init__(self, semaphores):
        self.semaphores = semaphores
        self.count = 0

    def start(self, source, target):
        copy = pltpu.make_async_copy(source, target, self.semaphores.at[self.count])
        self.count += 1
        copy.start()
        return copy

    def start_one(self, sources, chosen, target):
        slot = self.semaphores.at[self.count]
        self.count += 1
        for i, source in enumerate(sources):

            @pl.when(chosen == i)
            def _(source=source):
                pltpu.make_async_copy(source, target, slot).start()

        return pltpu.make_async_copy(sources[0], target, slot)


def clear(pad):
    slots, length, channels = pad.shape
    zeros = jnp.zeros((8, channels), jnp.float32)
    for slot in range(slots):
        pad[slot, 0:8] = zeros
        pad[slot, length - 8 : length] = zeros


def place(value, pad, slot):
    pad[slot, 8 : 8 + value.shape[0]] = value


def pack(kernel, out):
    channels = kernel.shape[2]
    zero = jnp.zeros((channels, channels), jnp.bfloat16)
    for j in range(4):
        for b in range(3):
            rows = pl.ds((3 * j + b) * channels, channels)
            out[rows, :channels] = kernel[j, b] if j < 3 else zero
            out[rows, channels:] = kernel[j - 1, b] if j > 0 else zero


def row_pair(pad, first, weights):
    columns = pad.shape[1] - 16
    lhs = [pad[first + j, 7 + b : 7 + b + columns] for j in range(4) for b in range(3)]
    lhs = jnp.concatenate(lhs, axis=-1).astype(jnp.bfloat16)
    return jnp.dot(lhs, weights[...], preferred_element_type=jnp.float32)


def ask(norm, slots, query_weight, key_weight, tempers, rows_of, query):
    channels = norm.shape[-1]
    mixing = lax.dot_general(
        query_weight[...],
        key_weight[...],
        (((1,), (1,)), ((), ())),
        preferred_element_type=jnp.float32,
    ).astype(jnp.bfloat16)
    scales = tempers[...].T * (math.log2(math.e) / math.sqrt(channels))
    for slot in range(slots):
        mixed = jnp.dot(norm[slot], mixing, preferred_element_type=jnp.float32)
        r = rows_of(slot)
        query[slot] = (mixed * scales[:, r : r + 1]).astype(jnp.bfloat16)


def middle_body(
    cells, one, two, query_weight, key_weight, tempers, gain,
    state_one_out, state_out, norm_out, query_out,
    held, one_held, two_held, query_held, key_held, tempers_held, gain_held,
    w1, w2, state_one, state_two, norm, query, x1, x2, sems,
):
    rows = cells.shape[0]
    channels = cells.shape[2]
    copies = Copies(sems)
    loads = [copies.start(cells.at[r], held.at[r]) for r in range(4)]
    later = [copies.start(one, one_held)]
    later += [copies.start(cells.at[r], held.at[r]) for r in range(4, rows)]
    later += [
        copies.start(two, two_held),
        copies.start(gain, gain_held),
        copies.start(query_weight, query_held),
        copies.start(key_weight, key_held),
        copies.start(tempers, tempers_held),
    ]
    clear(x1)
    clear(x2)

    def convolve_one(first):
        out = row_pair(x1, first, w1)
        for o in range(2):
            r = first + 1 + o
            state = held[r] + out[:, o * channels : (o + 1) * channels]
            state_one[r - 1] = state
            place(silu(state), x2, r - 1)

    def convolve_two(first):
        out = row_pair(x2, first, w2)
        for o in range(2):
            slot = first + o
            state = state_one[slot + 1] + out[:, o * channels : (o + 1) * channels]
            state_two[slot] = state
            norm[slot] = scaled(state, gain_held[...]).astype(jnp.bfloat16)

    for load in loads:
        load.wait()
    for r in range(4):
        place(silu(held[r]), x1, r)
    for load in later:
        load.wait()
    pack(one_held, w1)
    pack(two_held, w2)
    for first in range(0, rows - 2, 2):
        convolve_one(first)
        for r in range(first + 4, min(first + 6, rows)):
            place(silu(held[r]), x1, r)
        if first >= 2:
            convolve_two(first - 2)
    stores = [
        copies.start(norm, norm_out),
        copies.start(state_one.at[pl.ds(0, 2)], state_one_out.at[pl.ds(0, 2)]),
        copies.start(state_one.at[pl.ds(rows - 4, 2)], state_one_out.at[pl.ds(2, 2)]),
        copies.start(state_two, state_out),
    ]
    ask(norm, rows - 4, query_held, key_held, tempers_held, lambda slot: slot + 2, query)
    stores.append(copies.start(query, query_out))
    for store in stores:
        store.wait()


def scratch(*arrays):
    return [pltpu.VMEM(shape, kind) for shape, kind in arrays]


def middle_rows(cells, one, two, query_weight, key_weight, tempers, gain):
    rows, columns, channels = cells.shape
    row = (columns, channels)
    padded = (columns + 16, channels)
    packed = ((12 * channels, 2 * channels), jnp.bfloat16)
    operands = (cells, one, two, query_weight, key_weight, tempers, gain)
    return pl.pallas_call(
        middle_body,
        in_specs=[anywhere] * 7,
        out_specs=[anywhere] * 4,
        out_shape=[
            jax.ShapeDtypeStruct((4, *row), jnp.float32),
            jax.ShapeDtypeStruct((rows - 4, *row), jnp.float32),
            jax.ShapeDtypeStruct((rows - 4, *row), jnp.bfloat16),
            jax.ShapeDtypeStruct((rows - 4, *row), jnp.bfloat16),
        ],
        scratch_shapes=[
            *scratch(*[(a.shape, a.dtype) for a in operands]),
            *scratch(
                packed,
                packed,
                ((rows - 2, *row), jnp.float32),
                ((rows - 4, *row), jnp.float32),
                ((rows - 4, *row), jnp.bfloat16),
                ((rows - 4, *row), jnp.bfloat16),
                ((rows, *padded), jnp.float32),
                ((rows - 2, *padded), jnp.float32),
            ),
            pltpu.SemaphoreType.DMA((rows + 11,)),
        ],
        compiler_params=pltpu.CompilerParams(vmem_limit_bytes=whole_vmem_bytes),
        cost_estimate=no_cost,
        name="residual_middle",
    )(*operands)


def edge_body(
    cells, mate, cross, one, two, state_one, query_weight, key_weight, tempers, gain,
    state_out, norm_out, query_out,
    held, one_held, two_held, state_held, query_held, key_held,
    tempers_held, gain_held, w1, w2, state_two, norm, query, x1, x2, sems,
):
    rows = cells.shape[0]
    channels = cells.shape[2]
    first_band, last_band, odd = band_place()
    copies = Copies(sems)
    loads = [
        copies.start(cells.at[pl.ds(0, 2)], held.at[pl.ds(0, 2)]),
        copies.start(cells.at[pl.ds(rows - 2, 2)], held.at[pl.ds(2, 2)]),
    ]
    later = [
        copies.start(one, one_held),
        copies.start(two, two_held),
        copies.start(state_one, state_held),
        copies.start(query_weight, query_held),
        copies.start(key_weight, key_held),
        copies.start(tempers, tempers_held),
        copies.start(gain, gain_held),
    ]
    clear(x1)
    clear(x2)
    for load in loads:
        load.wait()
    for r in range(2):
        place(silu(held[r]), x1, 2 + r)
        place(silu(held[2 + r]), x1, 4 + r)
    outside = []
    for r in range(2):
        mate_row = mate[r].astype(jnp.float32)
        cross_row = cross[r].astype(jnp.float32)
        over = jnp.where(first_band, 0.0, jnp.where(odd, mate_row, cross_row))
        under = jnp.where(last_band, 0.0, jnp.where(odd, cross_row, mate_row))
        place(silu(over), x1, r)
        place(silu(under), x1, 6 + r)
        outside.append((over, under))
    over, under = outside[1][0], outside[0][1]
    for load in later:
        load.wait()
    pack(one_held, w1)
    pack(two_held, w2)
    out = row_pair(x1, 0, w1)
    over = over + out[:, :channels]
    top = held[0] + out[:, channels:]
    out = row_pair(x1, 4, w1)
    bottom = held[3] + out[:, :channels]
    under = under + out[:, channels:]
    for r in range(2):
        place(silu(state_held[r]), x2, 2 + r)
        place(silu(state_held[2 + r]), x2, 4 + r)
    place(jnp.where(first_band, 0.0, silu(over)), x2, 0)
    place(silu(top), x2, 1)
    place(silu(bottom), x2, 6)
    place(jnp.where(last_band, 0.0, silu(under)), x2, 7)
    for slot, states in ((0, (top, state_held[0])), (2, (state_held[3], bottom))):
        out = row_pair(x2, 2 * slot, w2)
        for o in range(2):
            state = states[o] + out[:, o * channels : (o + 1) * channels]
            state_two[slot + o] = state
            norm[slot + o] = scaled(state, gain_held[...]).astype(jnp.bfloat16)
    stores = [copies.start(norm, norm_out), copies.start(state_two, state_out)]
    ask(
        norm, 4, query_held, key_held, tempers_held,
        lambda slot: slot if slot < 2 else rows - 4 + slot, query,
    )
    stores.append(copies.start(query, query_out))
    for store in stores:
        store.wait()


def edge_rows(cells, mate, cross, one, two, state_one, query_weight, key_weight, tempers, gain):
    columns, channels = cells.shape[1:]
    row = (columns, channels)
    padded = (columns + 16, channels)
    packed = ((12 * channels, 2 * channels), jnp.bfloat16)
    operands = (
        cells, mate, cross, one, two, state_one, query_weight, key_weight, tempers, gain
    )
    return pl.pallas_call(
        edge_body,
        in_specs=[anywhere] + [in_vmem] * 2 + [anywhere] * 7,
        out_specs=[anywhere] * 3,
        out_shape=[
            jax.ShapeDtypeStruct((4, *row), jnp.float32),
            jax.ShapeDtypeStruct((4, *row), jnp.bfloat16),
            jax.ShapeDtypeStruct((4, *row), jnp.bfloat16),
        ],
        scratch_shapes=[
            *scratch(((4, *row), jnp.float32), *[(a.shape, a.dtype) for a in operands[3:]]),
            *scratch(
                packed,
                packed,
                ((4, *row), jnp.float32),
                ((4, *row), jnp.bfloat16),
                ((4, *row), jnp.bfloat16),
                ((8, *padded), jnp.float32),
                ((8, *padded), jnp.float32),
            ),
            pltpu.SemaphoreType.DMA((14,)),
        ],
        compiler_params=pltpu.CompilerParams(vmem_limit_bytes=whole_vmem_bytes),
        cost_estimate=no_cost,
        name="residual_edge",
    )(*operands)


def band_place():
    band = lax.axis_index("band")
    return band == 0, band == lax.axis_size("band") - 1, lax.rem(band, 2) == 1


def blend(query, window, store):
    keys, channels = window.shape
    extended = jnp.concatenate([window, jnp.ones((keys, channels), jnp.bfloat16)], axis=1)
    columns = query.shape[0]
    block = 128 if columns % 128 == 0 else columns
    for start in range(0, columns, block):
        scores = lax.dot_general(
            query[pl.ds(start, block)],
            window,
            (((1,), (1,)), ((), ())),
            preferred_element_type=jnp.float32,
        )
        peak = jnp.max(scores, axis=-1, keepdims=True)
        lifted = jnp.exp2(scores - peak).astype(jnp.bfloat16)
        total = jnp.dot(lifted, extended, preferred_element_type=jnp.float32)
        store(pl.ds(start, block), total[:, :channels] / total[:, channels:])


def pick(chosen, candidates):
    picked = candidates[0]
    for i, candidate in enumerate(candidates[1:], 1):
        picked = jnp.where(chosen == i, candidate, picked)
    return picked


def key_offset(partners, low, far):
    view = lax.axis_index("view")
    first = jnp.bitwise_xor(partners[view, 0], view)
    second = jnp.bitwise_xor(partners[view, 1], view)
    return (jnp.maximum(first, second) if far else jnp.minimum(first, second)) - low


def band_row(edge, middle, r):
    inner = middle.shape[0]
    if r < 2:
        return edge.at[r]
    if r < inner + 2:
        return middle.at[r - 2]
    return edge.at[r - inner]


def picked_row(chosen, edges, middles, r):
    return pick(chosen, [band_row(e, m, r)[...] for e, m in zip(edges, middles)])


def finish(r, both, state, value_out, gain, result):
    message = jnp.dot(both[r], value_out[...], preferred_element_type=jnp.float32)
    result[r] = state[...] + scaled(message, gain[...])


def take(refs, *counts):
    groups = []
    for count in counts:
        groups.append(refs[:count])
        refs = refs[count:]
    return (*groups, refs)


def gather_keys(chosen, edges, middles, keys):
    for r in range(keys.shape[0]):
        keys[r] = pick(chosen, [band_row(e, m, r)[...] for e, m in zip(edges, middles)])


def attend_near_body(low, count, partners, *refs):
    edges, middles, refs = take(refs, count, count)
    query_edge, query_middle, out, keys, held_edge, held_middle, sems = refs
    rows, columns, channels = keys.shape
    copies = Copies(sems)
    loads = [copies.start(query_edge, held_edge), copies.start(query_middle, held_middle)]
    gather_keys(key_offset(partners, low, False), edges, middles, keys)
    for load in loads:
        load.wait()
    for r in range(1, rows - 1):
        window = keys[r - 1 : r + 2].reshape(3 * columns, channels)

        def store(place, value, r=r):
            out[r - 1, place] = value.astype(jnp.bfloat16)

        blend(band_row(held_edge, held_middle, r), window, store)


def attend_far_body(low, count, partners, *refs):
    edges, middles, refs = take(refs, count, count)
    (
        query_edge, query_middle, near, state_edge, state_middle, value_out, gain,
        out, keys, both, result, sems,
    ) = refs
    rows, columns, channels = out.shape
    copies = Copies(sems)
    gather_keys(key_offset(partners, low, True), edges, middles, keys)
    for r in range(1, rows - 1):
        window = keys[r - 1 : r + 2].reshape(3 * columns, channels)

        def store(place, value, r=r):
            other = near[r - 1, place].astype(jnp.float32)
            both[r, place] = (value + other).astype(jnp.bfloat16)

        blend(band_row(query_edge, query_middle, r), window, store)
    for r in range(1, rows - 1):
        finish(r, both, band_row(state_edge, state_middle, r), value_out, gain, result)
    inner = pl.ds(1, rows - 2)
    copies.start(result.at[inner], out.at[inner]).wait()


def attend_outer_body(lows, counts, partners, *refs):
    near_count, far_count = counts
    near_edges, near_above, near_below, refs = take(refs, *[near_count] * 3)
    far_edges, far_above, far_below, refs = take(refs, *[far_count] * 3)
    query_edge, state_edge, value_out, gain, given, out, keys, both, result, sems = refs
    columns, channels = both.shape[1:]
    copies = Copies(sems)
    sides = (
        (key_offset(partners, lows[0], False), near_edges, near_above, near_below),
        (key_offset(partners, lows[1], True), far_edges, far_above, far_below),
    )
    for slot, (chosen, edges, above, below) in enumerate(sides):
        keys[6 * slot] = pick(chosen, [a[0] for a in above])
        keys[6 * slot + 5] = pick(chosen, [b[0] for b in below])
        for r in range(4):
            keys[6 * slot + 1 + r] = pick(chosen, [e[r] for e in edges])
    for slot in range(2):
        for end in range(2):
            first = 6 * slot + 3 * end
            window = keys[first : first + 3].reshape(3 * columns, channels)

            def store(place, value, slot=slot, end=end):
                if slot > 0:
                    value = value + both[end, place].astype(jnp.float32)
                both[end, place] = value.astype(jnp.bfloat16)

            blend(query_edge.at[3 * end], window, store)
    stores = []
    for end, r in ((0, 0), (1, out.shape[0] - 1)):
        finish(end, both, state_edge.at[3 * end], value_out, gain, result)
        stores.append(copies.start(result.at[end], out.at[r]))
    for store in stores:
        store.wait()


def attend_near(partners, low, candidates, queries):
    rows = candidates[0][0].shape[0] + candidates[1][0].shape[0]
    columns, channels = queries[0].shape[1:]
    operands = [a for group in candidates for a in group]
    return pl.pallas_call(
        functools.partial(attend_near_body, low, len(candidates[0])),
        in_specs=[in_smem] + [in_vmem] * len(operands) + [anywhere] * 2,
        out_specs=in_vmem,
        out_shape=jax.ShapeDtypeStruct((rows - 2, columns, channels), jnp.bfloat16),
        scratch_shapes=[
            pltpu.VMEM((rows, columns, channels), jnp.bfloat16),
            pltpu.VMEM(queries[0].shape, jnp.bfloat16),
            pltpu.VMEM(queries[1].shape, jnp.bfloat16),
            pltpu.SemaphoreType.DMA((2,)),
        ],
        compiler_params=pltpu.CompilerParams(vmem_limit_bytes=near_vmem_bytes),
        cost_estimate=no_cost,
        name="attend_near",
    )(partners, *operands, *queries)


def attend_far(partners, low, candidates, queries, near, states, value_out, gain):
    shape = (near.shape[0] + 2, *near.shape[1:])
    operands = [a for group in candidates for a in group]
    operands += [*queries, near, *states, value_out, gain]
    return pl.pallas_call(
        functools.partial(attend_far_body, low, len(candidates[0])),
        in_specs=[in_smem] + [in_vmem] * len(operands),
        out_specs=anywhere,
        out_shape=jax.ShapeDtypeStruct(shape, jnp.float32),
        scratch_shapes=[
            pltpu.VMEM(shape, jnp.bfloat16),
            pltpu.VMEM(shape, jnp.bfloat16),
            pltpu.VMEM(shape, jnp.float32),
            pltpu.SemaphoreType.DMA((1,)),
        ],
        compiler_params=pltpu.CompilerParams(vmem_limit_bytes=vmem_bytes),
        cost_estimate=no_cost,
        name="attend_far",
    )(partners, *operands)


def attend_outer(partners, lows, near_sides, far_sides, query, state, value_out, gain, given):
    columns, channels = query.shape[1:]
    operands = [a for group in near_sides + far_sides for a in group]
    operands += [query, state, value_out, gain]
    return pl.pallas_call(
        functools.partial(attend_outer_body, lows, (len(near_sides[0]), len(far_sides[0]))),
        in_specs=[in_smem] + [in_vmem] * len(operands) + [anywhere],
        out_specs=anywhere,
        out_shape=jax.ShapeDtypeStruct(given.shape, given.dtype),
        scratch_shapes=[
            pltpu.VMEM((12, columns, channels), jnp.bfloat16),
            pltpu.VMEM((2, columns, channels), jnp.bfloat16),
            pltpu.VMEM((2, columns, channels), jnp.float32),
            pltpu.SemaphoreType.DMA((2,)),
        ],
        input_output_aliases={1 + len(operands): 0},
        compiler_params=pltpu.CompilerParams(vmem_limit_bytes=vmem_bytes),
        cost_estimate=no_cost,
        name="attend_outer",
    )(partners, *operands, given)


def edge_halos_body(*refs):
    edges, (mate, cross) = refs[:-2], refs[-2:]
    odd = band_place()[2]
    for i, edge in enumerate(edges):
        mate[i] = jnp.where(odd, edge[0], edge[3])
        cross[i] = jnp.where(odd, edge[3], edge[0])


def edge_halos(edges):
    rows = jax.ShapeDtypeStruct((len(edges), *edges[0].shape[1:]), jnp.bfloat16)
    return pl.pallas_call(
        edge_halos_body,
        in_specs=[in_vmem] * len(edges),
        out_specs=[in_vmem] * 2,
        out_shape=[rows, rows],
        compiler_params=pltpu.CompilerParams(vmem_limit_bytes=vmem_bytes),
        cost_estimate=no_cost,
        name="edge_halos",
    )(*edges)


def outside_body(mate, cross, *outs):
    first_band, last_band, odd = band_place()
    for i in range(mate.shape[0]):
        above = jnp.where(odd, mate[i], cross[i])
        below = jnp.where(odd, cross[i], mate[i])
        outs[2 * i][0] = jnp.where(first_band, jnp.zeros_like(above), above)
        outs[2 * i + 1][0] = jnp.where(last_band, jnp.zeros_like(below), below)


def outside_rows(mate, cross):
    row = jax.ShapeDtypeStruct((1, *mate.shape[1:]), jnp.bfloat16)
    return pl.pallas_call(
        outside_body,
        in_specs=[in_vmem] * 2,
        out_specs=[in_vmem] * (2 * mate.shape[0]),
        out_shape=[row] * (2 * mate.shape[0]),
        compiler_params=pltpu.CompilerParams(vmem_limit_bytes=vmem_bytes),
        cost_estimate=no_cost,
        name="outside_rows",
    )(mate, cross)


def swap(cells, views, offset):
    return lax.ppermute(cells, "view", [(i, i ^ offset) for i in range(views)])


def gather_direct(cells, views):
    return {1 << i: swap(cells, views, 1 << i) for i in range((views - 1).bit_length())}


def relay(held, views, by_low):
    for offset in range(1, views):
        bit = offset & -offset if by_low else 1 << (offset.bit_length() - 1)
        if bit != offset:
            held[offset] = swap(held[offset ^ bit], views, bit)


def swap_bands(mate, cross, bands):
    mates = [(i, i ^ 1) for i in range(bands)]
    crosses = [(i, i + 1) for i in range(1, bands - 1, 2)]
    crosses = crosses + [(j, i) for i, j in crosses]
    return lax.ppermute(mate, "band", mates), lax.ppermute(cross, "band", crosses)


def per_device(
    features, tempers, partners, conv_one, conv_two, query_weight, key_weight,
    value_weight, out_weight, norm_gain, message_gain,
):
    views = lax.axis_size("view")
    bands = lax.axis_size("band")
    cells, temper, gain = features[0], tempers[0], norm_gain[None]

    state_one, state_middle, middle, query_middle = middle_rows(
        cells, conv_one, conv_two, query_weight, key_weight, temper, gain
    )
    middles = gather_direct(middle, views)
    head, tail = cells[:2].astype(jnp.bfloat16), cells[-2:].astype(jnp.bfloat16)
    odd = band_place()[2]
    mate, cross = swap_bands(
        jnp.where(odd, head, tail), jnp.where(odd, tail, head), bands
    )
    state_edge, edge, query_edge = edge_rows(
        cells, mate, cross, conv_one, conv_two, state_one, query_weight, key_weight, temper, gain
    )
    queries = (query_edge, query_middle)
    edges = gather_direct(edge, views)
    edges, middles = lax.optimization_barrier((edges, middles))
    direct = list(edges)
    halos = swap_bands(*edge_halos([edges[i] for i in direct]), bands)
    relay(edges, views, False)
    relay(middles, views, True)

    def candidates(groups, low, high):
        return [[group[i] for i in range(low, high + 1)] for group in groups]

    near_ends, far_ends = (1, max(1, views - 2)), (min(2, views - 1), views - 1)
    near = attend_near(partners, near_ends[0], candidates((edges, middles), *near_ends), queries)
    halos, near = lax.optimization_barrier((halos, near))
    halos = outside_rows(*halos)
    above = dict(zip(direct, halos[0::2]))
    below = dict(zip(direct, halos[1::2]))
    relay(above, views, True)
    relay(below, views, False)
    value_out = jnp.dot(value_weight, out_weight, preferred_element_type=jnp.float32).astype(
        jnp.bfloat16
    )
    rest = (value_out, message_gain[None])
    inner = attend_far(
        partners, far_ends[0], candidates((edges, middles), *far_ends), queries, near,
        (state_edge, state_middle), *rest,
    )
    sides = (edges, above, below)
    refined = attend_outer(
        partners, (near_ends[0], far_ends[0]), candidates(sides, *near_ends),
        candidates(sides, *far_ends), query_edge, state_edge, *rest, inner,
    )
    return refined[None]


def solution(mesh):
    whole = P()
    in_specs = (P("view", "band", None, None), P("view", "band", None)) + (whole,) * 9
    return jax.shard_map(
        per_device, mesh=mesh, in_specs=in_specs,
        out_specs=P("view", "band", None, None), check_vma=False,
    )
```

```python
import functools
import math

import jax
import jax.numpy as jnp
from jax import lax
from jax.experimental import pallas as pl
from jax.experimental.pallas import tpu as pltpu
from jax.sharding import PartitionSpec as P

epsilon = 1e-06
vmem_bytes = 28 * 1024 * 1024
edge_vmem_bytes = 36 * 1024 * 1024
whole_vmem_bytes = 56 * 1024 * 1024
in_vmem = pl.BlockSpec(memory_space=pltpu.VMEM)
in_smem = pl.BlockSpec(memory_space=pltpu.SMEM)
no_cost = pl.CostEstimate(flops=0, bytes_accessed=0, transcendentals=0)
anywhere = pl.BlockSpec(memory_space=pl.ANY)


def silu(v):
    half = 0.5 * v
    return half * jnp.tanh(half) + half


def scaled(values, gain):
    channels = values.shape[-1]
    squares = (values * values).astype(jnp.bfloat16)
    ones = jnp.ones((channels, channels), jnp.bfloat16)
    mean_square = jnp.dot(squares, ones, preferred_element_type=jnp.float32) * (1.0 / channels)
    return values * lax.rsqrt(mean_square + epsilon) * gain


class Copies:
    def __init__(self, semaphores):
        self.semaphores = semaphores
        self.count = 0

    def start(self, source, target):
        copy = pltpu.make_async_copy(source, target, self.semaphores.at[self.count])
        self.count += 1
        copy.start()
        return copy

    def start_one(self, sources, chosen, target):
        slot = self.semaphores.at[self.count]
        self.count += 1
        for i, source in enumerate(sources):

            @pl.when(chosen == i)
            def _(source=source):
                pltpu.make_async_copy(source, target, slot).start()

        return pltpu.make_async_copy(sources[0], target, slot)


def clear(pad):
    slots, length, channels = pad.shape
    zeros = jnp.zeros((8, channels), jnp.float32)
    for slot in range(slots):
        pad[slot, 0:8] = zeros
        pad[slot, length - 8 : length] = zeros


def place(value, pad, slot):
    pad[slot, 8 : 8 + value.shape[0]] = value


def pack(kernel, out):
    channels = kernel.shape[2]
    zero = jnp.zeros((channels, channels), jnp.bfloat16)
    for j in range(4):
        for b in range(3):
            rows = pl.ds((3 * j + b) * channels, channels)
            out[rows, :channels] = kernel[j, b] if j < 3 else zero
            out[rows, channels:] = kernel[j - 1, b] if j > 0 else zero


def row_pair(pad, first, weights):
    columns = pad.shape[1] - 16
    lhs = [pad[first + j, 7 + b : 7 + b + columns] for j in range(4) for b in range(3)]
    lhs = jnp.concatenate(lhs, axis=-1).astype(jnp.bfloat16)
    return jnp.dot(lhs, weights[...], preferred_element_type=jnp.float32)


def ask(norm, query_weight, key_weight, tempers, query_edge, query_middle):
    rows, channels = tempers.shape[0], norm[0].shape[-1]
    mixing = lax.dot_general(
        query_weight[...],
        key_weight[...],
        (((1,), (1,)), ((), ())),
        preferred_element_type=jnp.float32,
    ).astype(jnp.bfloat16)
    scales = tempers[...].T * (math.log2(math.e) / math.sqrt(channels))
    for r in range(rows):
        row = band_row(*norm, r)[...]
        mixed = jnp.dot(row, mixing, preferred_element_type=jnp.float32)
        query = (mixed * scales[:, r : r + 1]).astype(jnp.bfloat16)
        band_row(query_edge, query_middle, r)[...] = query


def middle_body(
    cells, one, two, gain, state_one_out, state_out, norm_out,
    held, one_held, two_held, gain_held, w1, w2, state_one, state_two, norm, x1, x2, sems,
):
    rows = cells.shape[0]
    channels = cells.shape[2]
    copies = Copies(sems)
    loads = [copies.start(cells.at[r], held.at[r]) for r in range(4)]
    later = [copies.start(one, one_held)]
    later += [copies.start(cells.at[r], held.at[r]) for r in range(4, rows)]
    later += [
        copies.start(two, two_held),
        copies.start(gain, gain_held),
    ]
    clear(x1)
    clear(x2)

    def convolve_one(first):
        out = row_pair(x1, first, w1)
        for o in range(2):
            r = first + 1 + o
            state = held[r] + out[:, o * channels : (o + 1) * channels]
            state_one[r - 1] = state
            place(silu(state), x2, r - 1)

    def convolve_two(first):
        out = row_pair(x2, first, w2)
        for o in range(2):
            slot = first + o
            state = state_one[slot + 1] + out[:, o * channels : (o + 1) * channels]
            state_two[slot] = state
            norm[slot] = scaled(state, gain_held[...]).astype(jnp.bfloat16)

    for load in loads:
        load.wait()
    for r in range(4):
        place(silu(held[r]), x1, r)
    for load in later:
        load.wait()
    pack(one_held, w1)
    pack(two_held, w2)
    for first in range(0, rows - 2, 2):
        convolve_one(first)
        for r in range(first + 4, min(first + 6, rows)):
            place(silu(held[r]), x1, r)
        if first >= 2:
            convolve_two(first - 2)
    stores = [
        copies.start(norm, norm_out),
        copies.start(state_one.at[pl.ds(0, 2)], state_one_out.at[pl.ds(0, 2)]),
        copies.start(state_one.at[pl.ds(rows - 4, 2)], state_one_out.at[pl.ds(2, 2)]),
        copies.start(state_two, state_out),
    ]
    for store in stores:
        store.wait()


def scratch(*arrays):
    return [pltpu.VMEM(shape, kind) for shape, kind in arrays]


def middle_rows(cells, one, two, gain):
    rows, columns, channels = cells.shape
    row = (columns, channels)
    padded = (columns + 16, channels)
    packed = ((12 * channels, 2 * channels), jnp.bfloat16)
    operands = (cells, one, two, gain)
    return pl.pallas_call(
        middle_body,
        in_specs=[anywhere] * 4,
        out_specs=[anywhere] * 3,
        out_shape=[
            jax.ShapeDtypeStruct((4, *row), jnp.float32),
            jax.ShapeDtypeStruct((rows - 4, *row), jnp.float32),
            jax.ShapeDtypeStruct((rows - 4, *row), jnp.bfloat16),
        ],
        scratch_shapes=[
            *scratch(*[(a.shape, a.dtype) for a in operands]),
            *scratch(
                packed,
                packed,
                ((rows - 2, *row), jnp.float32),
                ((rows - 4, *row), jnp.float32),
                ((rows - 4, *row), jnp.bfloat16),
                ((rows, *padded), jnp.float32),
                ((rows - 2, *padded), jnp.float32),
            ),
            pltpu.SemaphoreType.DMA((rows + 7,)),
        ],
        compiler_params=pltpu.CompilerParams(vmem_limit_bytes=whole_vmem_bytes),
        cost_estimate=no_cost,
        name="residual_middle",
    )(*operands)


def edge_body(
    cells, mate, cross, one, two, state_one, gain, state_out, norm_out,
    held, one_held, two_held, state_held, gain_held, w1, w2, state_two, norm, x1, x2, sems,
):
    rows = cells.shape[0]
    channels = cells.shape[2]
    first_band, last_band, odd = band_place()
    copies = Copies(sems)
    loads = [
        copies.start(cells.at[pl.ds(0, 2)], held.at[pl.ds(0, 2)]),
        copies.start(cells.at[pl.ds(rows - 2, 2)], held.at[pl.ds(2, 2)]),
    ]
    later = [
        copies.start(one, one_held),
        copies.start(two, two_held),
        copies.start(state_one, state_held),
        copies.start(gain, gain_held),
    ]
    clear(x1)
    clear(x2)
    for load in loads:
        load.wait()
    for r in range(2):
        place(silu(held[r]), x1, 2 + r)
        place(silu(held[2 + r]), x1, 4 + r)
    outside = []
    for r in range(2):
        mate_row = mate[r].astype(jnp.float32)
        cross_row = cross[r].astype(jnp.float32)
        over = jnp.where(first_band, 0.0, jnp.where(odd, mate_row, cross_row))
        under = jnp.where(last_band, 0.0, jnp.where(odd, cross_row, mate_row))
        place(silu(over), x1, r)
        place(silu(under), x1, 6 + r)
        outside.append((over, under))
    over, under = outside[1][0], outside[0][1]
    for load in later:
        load.wait()
    pack(one_held, w1)
    pack(two_held, w2)
    out = row_pair(x1, 0, w1)
    over = over + out[:, :channels]
    top = held[0] + out[:, channels:]
    out = row_pair(x1, 4, w1)
    bottom = held[3] + out[:, :channels]
    under = under + out[:, channels:]
    for r in range(2):
        place(silu(state_held[r]), x2, 2 + r)
        place(silu(state_held[2 + r]), x2, 4 + r)
    place(jnp.where(first_band, 0.0, silu(over)), x2, 0)
    place(silu(top), x2, 1)
    place(silu(bottom), x2, 6)
    place(jnp.where(last_band, 0.0, silu(under)), x2, 7)
    for slot, states in ((0, (top, state_held[0])), (2, (state_held[3], bottom))):
        out = row_pair(x2, 2 * slot, w2)
        for o in range(2):
            state = states[o] + out[:, o * channels : (o + 1) * channels]
            state_two[slot + o] = state
            norm[slot + o] = scaled(state, gain_held[...]).astype(jnp.bfloat16)
    stores = [copies.start(norm, norm_out), copies.start(state_two, state_out)]
    for store in stores:
        store.wait()


def edge_rows(cells, mate, cross, one, two, state_one, gain):
    columns, channels = cells.shape[1:]
    row = (columns, channels)
    padded = (columns + 16, channels)
    packed = ((12 * channels, 2 * channels), jnp.bfloat16)
    operands = (cells, mate, cross, one, two, state_one, gain)
    return pl.pallas_call(
        edge_body,
        in_specs=[anywhere] + [in_vmem] * 2 + [anywhere] * 4,
        out_specs=[anywhere] * 2,
        out_shape=[
            jax.ShapeDtypeStruct((4, *row), jnp.float32),
            jax.ShapeDtypeStruct((4, *row), jnp.bfloat16),
        ],
        scratch_shapes=[
            *scratch(((4, *row), jnp.float32), *[(a.shape, a.dtype) for a in operands[3:]]),
            *scratch(
                packed,
                packed,
                ((4, *row), jnp.float32),
                ((4, *row), jnp.bfloat16),
                ((8, *padded), jnp.float32),
                ((8, *padded), jnp.float32),
            ),
            pltpu.SemaphoreType.DMA((8,)),
        ],
        compiler_params=pltpu.CompilerParams(vmem_limit_bytes=edge_vmem_bytes),
        cost_estimate=no_cost,
        name="residual_edge",
    )(*operands)


def band_place():
    band = lax.axis_index("band")
    return band == 0, band == lax.axis_size("band") - 1, lax.rem(band, 2) == 1


def blend(query, window, store):
    keys, channels = window.shape
    extended = jnp.concatenate([window, jnp.ones((keys, channels), jnp.bfloat16)], axis=1)
    columns = query.shape[0]
    block = 128 if columns % 128 == 0 else columns
    for start in range(0, columns, block):
        scores = lax.dot_general(
            query[pl.ds(start, block)],
            window,
            (((1,), (1,)), ((), ())),
            preferred_element_type=jnp.float32,
        )
        peak = jnp.max(scores, axis=-1, keepdims=True)
        lifted = jnp.exp2(scores - peak).astype(jnp.bfloat16)
        total = jnp.dot(lifted, extended, preferred_element_type=jnp.float32)
        store(pl.ds(start, block), total[:, :channels] / total[:, channels:])


def pick(chosen, candidates):
    picked = candidates[0]
    for i, candidate in enumerate(candidates[1:], 1):
        picked = jnp.where(chosen == i, candidate, picked)
    return picked


def key_offset(partners, low, far):
    view = lax.axis_index("view")
    first = jnp.bitwise_xor(partners[view, 0], view)
    second = jnp.bitwise_xor(partners[view, 1], view)
    return (jnp.maximum(first, second) if far else jnp.minimum(first, second)) - low


def band_row(edge, middle, r):
    inner = middle.shape[0]
    if r < 2:
        return edge.at[r]
    if r < inner + 2:
        return middle.at[r - 2]
    return edge.at[r - inner]


def picked_row(chosen, edges, middles, r):
    return pick(chosen, [band_row(e, m, r)[...] for e, m in zip(edges, middles)])


def finish(r, both, state, value_out, gain, result):
    message = jnp.dot(both[r], value_out[...], preferred_element_type=jnp.float32)
    result[r] = state[...] + scaled(message, gain[...])


def take(refs, *counts):
    groups = []
    for count in counts:
        groups.append(refs[:count])
        refs = refs[count:]
    return (*groups, refs)


def gather_keys(chosen, edges, middles, keys):
    for r in range(keys.shape[0]):
        keys[r] = pick(chosen, [band_row(e, m, r)[...] for e, m in zip(edges, middles)])


def attend_first_body(low, count, partners, *refs):
    middles, refs = take(refs, count)
    (
        edge, middle, query_weight, key_weight, tempers, query_edge, query_middle, out, keys
    ) = refs
    ask((edge, middle), query_weight, key_weight, tempers, query_edge, query_middle)
    columns, channels = out.shape[1:]
    chosen = key_offset(partners, low, False)
    for r in range(keys.shape[0]):
        keys[r] = pick(chosen, [m[r] for m in middles])
    for r in range(out.shape[0]):
        window = keys[r : r + 3].reshape(3 * columns, channels)

        def store(place, value, r=r):
            out[r, place] = value.astype(jnp.bfloat16)

        blend(query_middle.at[r + 1], window, store)


def attend_near_body(low, count, partners, *refs):
    edges, middles, refs = take(refs, count, count)
    query_edge, query_middle, out, keys = refs
    rows, columns, channels = keys.shape
    gather_keys(key_offset(partners, low, False), edges, middles, keys)
    for slot, r in enumerate((1, 2, rows - 3, rows - 2)):
        window = keys[r - 1 : r + 2].reshape(3 * columns, channels)

        def store(place, value, slot=slot):
            out[slot, place] = value.astype(jnp.bfloat16)

        blend(band_row(query_edge, query_middle, r), window, store)


def attend_far_body(low, count, partners, *refs):
    edges, middles, refs = take(refs, count, count)
    (
        query_edge, query_middle, near, first, state_edge, state_middle, value_out, gain,
        out, keys, both,
    ) = refs
    rows, columns, channels = keys.shape
    gather_keys(key_offset(partners, low, True), edges, middles, keys)
    for r in range(1, rows - 1):
        window = keys[r - 1 : r + 2].reshape(3 * columns, channels)
        other = band_row(near, first, r - 1)

        def store(place, value, r=r, other=other):
            both[r - 1, place] = (value + other[place].astype(jnp.float32)).astype(jnp.bfloat16)

        blend(band_row(query_edge, query_middle, r), window, store)
    for r in range(1, rows - 1):
        finish(r - 1, both, band_row(state_edge, state_middle, r), value_out, gain, out)


def end_windows(chosen, edges, above, below, keys):
    keys[0] = above
    keys[5] = below
    for r in range(4):
        keys[1 + r] = pick(chosen, [e[r] for e in edges])


def attend_ends_body(low, count, partners, *refs):
    edges, refs = take(refs, count)
    mate, cross, query_edge, out = refs[:4]
    outs, keys = refs[4:-1], refs[-1]
    columns, channels = out.shape[1:]
    first_band, last_band, odd = band_place()
    for i in range(mate.shape[0]):
        above = jnp.where(odd, mate[i], cross[i])
        below = jnp.where(odd, cross[i], mate[i])
        outs[2 * i][0] = jnp.where(first_band, jnp.zeros_like(above), above)
        outs[2 * i + 1][0] = jnp.where(last_band, jnp.zeros_like(below), below)
    chosen = key_offset(partners, low, False)
    above = pick(chosen, [a[0] for a in outs[0::2]])
    below = pick(chosen, [b[0] for b in outs[1::2]])
    end_windows(chosen, edges, above, below, keys)
    for end in range(2):
        window = keys[3 * end : 3 * end + 3].reshape(3 * columns, channels)

        def store(place, value, end=end):
            out[end, place] = value.astype(jnp.bfloat16)

        blend(query_edge.at[3 * end], window, store)


def attend_outer_body(low, count, partners, *refs):
    edges, aboves, belows, refs = take(refs, count, count, count)
    query_edge, ends, state_edge, value_out, gain, inner, out, keys, both, result, sems = refs
    rows, columns, channels = out.shape
    copies = Copies(sems)
    stores = [copies.start(inner, out.at[pl.ds(1, rows - 2)])]
    chosen = key_offset(partners, low, True)
    above = pick(chosen, [a[0] for a in aboves])
    below = pick(chosen, [b[0] for b in belows])
    end_windows(chosen, edges, above, below, keys)
    for end in range(2):
        window = keys[3 * end : 3 * end + 3].reshape(3 * columns, channels)

        def store(place, value, end=end):
            both[end, place] = (value + ends[end, place].astype(jnp.float32)).astype(jnp.bfloat16)

        blend(query_edge.at[3 * end], window, store)
    for end in range(2):
        finish(end, both, state_edge.at[3 * end], value_out, gain, result)
    stores += [copies.start(result.at[0], out.at[0]), copies.start(result.at[1], out.at[rows - 1])]
    for store in stores:
        store.wait()


def attend_first(partners, low, middles, edge, middle, query_weight, key_weight, tempers):
    rows, columns = tempers.shape
    channels = edge.shape[-1]
    operands = [*middles, edge, middle, query_weight, key_weight, tempers]
    like = jax.ShapeDtypeStruct
    return pl.pallas_call(
        functools.partial(attend_first_body, low, len(middles)),
        in_specs=[in_smem] + [in_vmem] * len(operands),
        out_specs=[in_vmem] * 3,
        out_shape=[
            like(edge.shape, jnp.bfloat16),
            like(middle.shape, jnp.bfloat16),
            like((rows - 6, columns, channels), jnp.bfloat16),
        ],
        scratch_shapes=[pltpu.VMEM(middle.shape, jnp.bfloat16)],
        compiler_params=pltpu.CompilerParams(vmem_limit_bytes=vmem_bytes),
        cost_estimate=no_cost,
        name="attend_first",
    )(partners, *operands)


def attend_near(partners, low, candidates, queries):
    rows = candidates[0][0].shape[0] + candidates[1][0].shape[0]
    columns, channels = queries[0].shape[1:]
    operands = [a for group in candidates for a in group] + list(queries)
    return pl.pallas_call(
        functools.partial(attend_near_body, low, len(candidates[0])),
        in_specs=[in_smem] + [in_vmem] * len(operands),
        out_specs=in_vmem,
        out_shape=jax.ShapeDtypeStruct((4, columns, channels), jnp.bfloat16),
        scratch_shapes=[pltpu.VMEM((rows, columns, channels), jnp.bfloat16)],
        compiler_params=pltpu.CompilerParams(vmem_limit_bytes=vmem_bytes),
        cost_estimate=no_cost,
        name="attend_near",
    )(partners, *operands)


def attend_far(partners, low, candidates, queries, near, first, states, value_out, gain):
    columns, channels = near.shape[1:]
    rows = near.shape[0] + first.shape[0]
    operands = [a for group in candidates for a in group]
    operands += [*queries, near, first, *states, value_out, gain]
    return pl.pallas_call(
        functools.partial(attend_far_body, low, len(candidates[0])),
        in_specs=[in_smem] + [in_vmem] * len(operands),
        out_specs=in_vmem,
        out_shape=jax.ShapeDtypeStruct((rows, columns, channels), jnp.float32),
        scratch_shapes=[
            pltpu.VMEM((rows + 2, columns, channels), jnp.bfloat16),
            pltpu.VMEM((rows, columns, channels), jnp.bfloat16),
        ],
        compiler_params=pltpu.CompilerParams(vmem_limit_bytes=vmem_bytes),
        cost_estimate=no_cost,
        name="attend_far",
    )(partners, *operands)


def attend_ends(partners, low, edges, mate, cross, query):
    columns, channels = query.shape[1:]
    row = jax.ShapeDtypeStruct((1, columns, channels), jnp.bfloat16)
    operands = [*edges, mate, cross, query]
    return pl.pallas_call(
        functools.partial(attend_ends_body, low, len(edges)),
        in_specs=[in_smem] + [in_vmem] * len(operands),
        out_specs=[in_vmem] * (1 + 2 * mate.shape[0]),
        out_shape=[jax.ShapeDtypeStruct((2, columns, channels), jnp.bfloat16)]
        + [row] * (2 * mate.shape[0]),
        scratch_shapes=[pltpu.VMEM((6, columns, channels), jnp.bfloat16)],
        compiler_params=pltpu.CompilerParams(vmem_limit_bytes=vmem_bytes),
        cost_estimate=no_cost,
        name="attend_ends",
    )(partners, *operands)


def attend_outer(partners, low, sides, query, ends, state, value_out, gain, inner):
    rows, columns, channels = inner.shape
    operands = [a for group in sides for a in group]
    operands += [query, ends, state, value_out, gain, inner]
    return pl.pallas_call(
        functools.partial(attend_outer_body, low, len(sides[0])),
        in_specs=[in_smem] + [in_vmem] * len(operands),
        out_specs=anywhere,
        out_shape=jax.ShapeDtypeStruct((rows + 2, columns, channels), jnp.float32),
        scratch_shapes=[
            pltpu.VMEM((6, columns, channels), jnp.bfloat16),
            pltpu.VMEM((2, columns, channels), jnp.bfloat16),
            pltpu.VMEM((2, columns, channels), jnp.float32),
            pltpu.SemaphoreType.DMA((3,)),
        ],
        compiler_params=pltpu.CompilerParams(vmem_limit_bytes=vmem_bytes),
        cost_estimate=no_cost,
        name="attend_outer",
    )(partners, *operands)


def edge_halos_body(*refs):
    edges, (mate, cross) = refs[:-2], refs[-2:]
    odd = band_place()[2]
    for i, edge in enumerate(edges):
        mate[i] = jnp.where(odd, edge[0], edge[3])
        cross[i] = jnp.where(odd, edge[3], edge[0])


def edge_halos(edges):
    rows = jax.ShapeDtypeStruct((len(edges), *edges[0].shape[1:]), jnp.bfloat16)
    return pl.pallas_call(
        edge_halos_body,
        in_specs=[in_vmem] * len(edges),
        out_specs=[in_vmem] * 2,
        out_shape=[rows, rows],
        compiler_params=pltpu.CompilerParams(vmem_limit_bytes=vmem_bytes),
        cost_estimate=no_cost,
        name="edge_halos",
    )(*edges)


def swap(cells, views, offset):
    return lax.ppermute(cells, "view", [(i, i ^ offset) for i in range(views)])


def gather_direct(cells, views):
    return {1 << i: swap(cells, views, 1 << i) for i in range((views - 1).bit_length())}


def relay(held, views, by_low):
    for offset in range(1, views):
        bit = offset & -offset if by_low else 1 << (offset.bit_length() - 1)
        if bit != offset:
            held[offset] = swap(held[offset ^ bit], views, bit)


def swap_bands(mate, cross, bands):
    mates = [(i, i ^ 1) for i in range(bands)]
    crosses = [(i, i + 1) for i in range(1, bands - 1, 2)]
    crosses = crosses + [(j, i) for i, j in crosses]
    return lax.ppermute(mate, "band", mates), lax.ppermute(cross, "band", crosses)


def per_device(
    features, tempers, partners, conv_one, conv_two, query_weight, key_weight,
    value_weight, out_weight, norm_gain, message_gain,
):
    views = lax.axis_size("view")
    bands = lax.axis_size("band")
    cells, temper, gain = features[0], tempers[0], norm_gain[None]

    state_one, state_middle, middle = middle_rows(cells, conv_one, conv_two, gain)
    middles = gather_direct(middle, views)
    halo_cells, middle = lax.optimization_barrier((cells, middle))
    head, tail = halo_cells[:2].astype(jnp.bfloat16), halo_cells[-2:].astype(jnp.bfloat16)
    odd = band_place()[2]
    mate, cross = swap_bands(jnp.where(odd, head, tail), jnp.where(odd, tail, head), bands)
    state_edge, edge = edge_rows(cells, mate, cross, conv_one, conv_two, state_one, gain)
    edges = gather_direct(edge, views)

    def candidates(groups, low, high):
        return [[group[i] for i in range(low, high + 1)] for group in groups]

    near_ends, far_ends = (1, max(1, views - 2)), (min(2, views - 1), views - 1)
    direct = list(edges)
    *queries, first = attend_first(
        partners, 1, [middles[i] for i in direct], edge, middle, query_weight, key_weight, temper
    )
    value_out = jnp.dot(value_weight, out_weight, preferred_element_type=jnp.float32).astype(
        jnp.bfloat16
    )
    edges, middles, queries, first, value_out = lax.optimization_barrier(
        (edges, middles, queries, first, value_out)
    )
    mate, cross = swap_bands(*edge_halos([edges[i] for i in direct]), bands)
    relay(edges, views, False)
    relay(middles, views, True)
    near = attend_near(partners, near_ends[0], candidates((edges, middles), *near_ends), queries)
    mate, cross, near = lax.optimization_barrier((mate, cross, near))
    near_edges = candidates((edges,), *near_ends)[0]
    ends, *halos = attend_ends(partners, near_ends[0], near_edges, mate, cross, queries[0])
    edges, middles, halos, ends = lax.optimization_barrier((edges, middles, halos, ends))
    above = dict(zip(direct, halos[0::2]))
    below = dict(zip(direct, halos[1::2]))
    relay(above, views, True)
    relay(below, views, False)
    rest = (value_out, message_gain[None])
    inner = attend_far(
        partners, far_ends[0], candidates((edges, middles), *far_ends), queries, near, first,
        (state_edge, state_middle), *rest,
    )
    refined = attend_outer(
        partners, far_ends[0], candidates((edges, above, below), *far_ends), queries[0], ends,
        state_edge, *rest, inner,
    )
    return refined[None]


def solution(mesh):
    whole = P()
    in_specs = (P("view", "band", None, None), P("view", "band", None)) + (whole,) * 9
    return jax.shard_map(
        per_device, mesh=mesh, in_specs=in_specs,
        out_specs=P("view", "band", None, None), check_vma=False,
    )
```

```python
import functools
import math

import jax
import jax.numpy as jnp
from jax import lax
from jax.experimental import pallas as pl
from jax.experimental.pallas import tpu as pltpu
from jax.sharding import PartitionSpec as P

epsilon = 1e-06
vmem_bytes = 28 * 1024 * 1024
edge_vmem_bytes = 50 * 1024 * 1024
whole_vmem_bytes = 56 * 1024 * 1024
in_vmem = pl.BlockSpec(memory_space=pltpu.VMEM)
in_smem = pl.BlockSpec(memory_space=pltpu.SMEM)
no_cost = pl.CostEstimate(flops=0, bytes_accessed=0, transcendentals=0)
anywhere = pl.BlockSpec(memory_space=pl.ANY)


def silu(v):
    half = 0.5 * v
    return half * jnp.tanh(half) + half


def scaled(values, gain):
    mean_square = jnp.mean(values * values, axis=-1, keepdims=True)
    return values * lax.rsqrt(mean_square + epsilon) * gain


class Copies:
    def __init__(self, semaphores):
        self.semaphores = semaphores
        self.count = 0

    def start(self, source, target):
        copy = pltpu.make_async_copy(source, target, self.semaphores.at[self.count])
        self.count += 1
        copy.start()
        return copy

    def start_one(self, sources, chosen, target):
        slot = self.semaphores.at[self.count]
        self.count += 1
        for i, source in enumerate(sources):

            @pl.when(chosen == i)
            def _(source=source):
                pltpu.make_async_copy(source, target, slot).start()

        return pltpu.make_async_copy(sources[0], target, slot)


def clear(pad):
    slots, length, channels = pad.shape
    zeros = jnp.zeros((8, channels), jnp.float32)
    for slot in range(slots):
        pad[slot, 0:8] = zeros
        pad[slot, length - 8 : length] = zeros


def place(value, pad, slot):
    pad[slot, 8 : 8 + value.shape[0]] = value


def pack(kernel, out):
    channels = kernel.shape[2]
    zero = jnp.zeros((channels, channels), jnp.bfloat16)
    for j in range(4):
        for b in range(3):
            rows = pl.ds((3 * j + b) * channels, channels)
            out[rows, :channels] = kernel[j, b] if j < 3 else zero
            out[rows, channels:] = kernel[j - 1, b] if j > 0 else zero


def row_pair(pad, first, weights):
    columns = pad.shape[1] - 16
    lhs = [pad[first + j, 7 + b : 7 + b + columns] for j in range(4) for b in range(3)]
    lhs = jnp.concatenate(lhs, axis=-1).astype(jnp.bfloat16)
    return jnp.dot(lhs, weights[...], preferred_element_type=jnp.float32)


def ask(norm, query_weight, key_weight, tempers, query_edge, query_middle):
    rows, channels = tempers.shape[0], norm[0].shape[-1]
    mixing = lax.dot_general(
        query_weight[...],
        key_weight[...],
        (((1,), (1,)), ((), ())),
        preferred_element_type=jnp.float32,
    ).astype(jnp.bfloat16)
    scales = tempers[...].T * (math.log2(math.e) / math.sqrt(channels))
    for r in range(rows):
        row = band_row(*norm, r)[...]
        mixed = jnp.dot(row, mixing, preferred_element_type=jnp.float32)
        query = (mixed * scales[:, r : r + 1]).astype(jnp.bfloat16)
        band_row(query_edge, query_middle, r)[...] = query


def middle_body(
    cells, one, two, gain, state_one_out, state_out, norm_out,
    held, one_held, two_held, gain_held, w1, w2, state_one, state_two, norm, x1, x2, sems,
):
    rows = cells.shape[0]
    channels = cells.shape[2]
    copies = Copies(sems)
    loads = [copies.start(cells.at[r], held.at[r]) for r in range(4)]
    later = [copies.start(one, one_held)]
    later += [copies.start(cells.at[r], held.at[r]) for r in range(4, rows)]
    later += [
        copies.start(two, two_held),
        copies.start(gain, gain_held),
    ]
    clear(x1)
    clear(x2)

    def convolve_one(first):
        out = row_pair(x1, first, w1)
        for o in range(2):
            r = first + 1 + o
            state = held[r] + out[:, o * channels : (o + 1) * channels]
            state_one[r - 1] = state
            place(silu(state), x2, r - 1)

    def convolve_two(first):
        out = row_pair(x2, first, w2)
        for o in range(2):
            slot = first + o
            state = state_one[slot + 1] + out[:, o * channels : (o + 1) * channels]
            state_two[slot] = state
            norm[slot] = scaled(state, gain_held[...]).astype(jnp.bfloat16)

    for load in loads:
        load.wait()
    for r in range(4):
        place(silu(held[r]), x1, r)
    for load in later:
        load.wait()
    pack(one_held, w1)
    pack(two_held, w2)
    for first in range(0, rows - 2, 2):
        convolve_one(first)
        for r in range(first + 4, min(first + 6, rows)):
            place(silu(held[r]), x1, r)
        if 2 <= first < rows - 4:
            convolve_two(first - 2)
    stores = [
        copies.start(state_one.at[pl.ds(0, 2)], state_one_out.at[pl.ds(0, 2)]),
        copies.start(state_one.at[pl.ds(rows - 4, 2)], state_one_out.at[pl.ds(2, 2)]),
        copies.start(norm.at[pl.ds(0, rows - 6)], norm_out.at[pl.ds(0, rows - 6)]),
        copies.start(state_two.at[pl.ds(0, rows - 6)], state_out.at[pl.ds(0, rows - 6)]),
    ]
    convolve_two(rows - 6)
    last = pl.ds(rows - 6, 2)
    stores += [
        copies.start(norm.at[last], norm_out.at[last]),
        copies.start(state_two.at[last], state_out.at[last]),
    ]
    for store in stores:
        store.wait()


def scratch(*arrays):
    return [pltpu.VMEM(shape, kind) for shape, kind in arrays]


def middle_rows(cells, one, two, gain):
    rows, columns, channels = cells.shape
    row = (columns, channels)
    padded = (columns + 16, channels)
    packed = ((12 * channels, 2 * channels), jnp.bfloat16)
    operands = (cells, one, two, gain)
    return pl.pallas_call(
        middle_body,
        in_specs=[anywhere] * 4,
        out_specs=[anywhere] * 3,
        out_shape=[
            jax.ShapeDtypeStruct((4, *row), jnp.float32),
            jax.ShapeDtypeStruct((rows - 4, *row), jnp.float32),
            jax.ShapeDtypeStruct((rows - 4, *row), jnp.bfloat16),
        ],
        scratch_shapes=[
            *scratch(*[(a.shape, a.dtype) for a in operands]),
            *scratch(
                packed,
                packed,
                ((rows - 2, *row), jnp.float32),
                ((rows - 4, *row), jnp.float32),
                ((rows - 4, *row), jnp.bfloat16),
                ((rows, *padded), jnp.float32),
                ((rows - 2, *padded), jnp.float32),
            ),
            pltpu.SemaphoreType.DMA((rows + 9,)),
        ],
        compiler_params=pltpu.CompilerParams(vmem_limit_bytes=whole_vmem_bytes),
        cost_estimate=no_cost,
        name="residual_middle",
    )(*operands)


def edge_body(
    cells, mate, cross, one, two, state_one, gain, state_out, norm_out,
    held, one_held, two_held, state_held, gain_held, w1, w2, state_two, norm, x1, x2, sems,
):
    rows = cells.shape[0]
    channels = cells.shape[2]
    first_band, last_band, odd = band_place()
    copies = Copies(sems)
    loads = [
        copies.start(cells.at[pl.ds(0, 2)], held.at[pl.ds(0, 2)]),
        copies.start(cells.at[pl.ds(rows - 2, 2)], held.at[pl.ds(2, 2)]),
    ]
    later = [
        copies.start(one, one_held),
        copies.start(two, two_held),
        copies.start(state_one, state_held),
        copies.start(gain, gain_held),
    ]
    clear(x1)
    clear(x2)
    for load in loads:
        load.wait()
    for r in range(2):
        place(silu(held[r]), x1, 2 + r)
        place(silu(held[2 + r]), x1, 4 + r)
    outside = []
    for r in range(2):
        mate_row = mate[r].astype(jnp.float32)
        cross_row = cross[r].astype(jnp.float32)
        over = jnp.where(first_band, 0.0, jnp.where(odd, mate_row, cross_row))
        under = jnp.where(last_band, 0.0, jnp.where(odd, cross_row, mate_row))
        place(silu(over), x1, r)
        place(silu(under), x1, 6 + r)
        outside.append((over, under))
    over, under = outside[1][0], outside[0][1]
    for load in later:
        load.wait()
    pack(one_held, w1)
    pack(two_held, w2)
    out = row_pair(x1, 0, w1)
    over = over + out[:, :channels]
    top = held[0] + out[:, channels:]
    out = row_pair(x1, 4, w1)
    bottom = held[3] + out[:, :channels]
    under = under + out[:, channels:]
    for r in range(2):
        place(silu(state_held[r]), x2, 2 + r)
        place(silu(state_held[2 + r]), x2, 4 + r)
    place(jnp.where(first_band, 0.0, silu(over)), x2, 0)
    place(silu(top), x2, 1)
    place(silu(bottom), x2, 6)
    place(jnp.where(last_band, 0.0, silu(under)), x2, 7)
    for slot, states in ((0, (top, state_held[0])), (2, (state_held[3], bottom))):
        out = row_pair(x2, 2 * slot, w2)
        for o in range(2):
            state = states[o] + out[:, o * channels : (o + 1) * channels]
            state_two[slot + o] = state
            norm[slot + o] = scaled(state, gain_held[...]).astype(jnp.bfloat16)
    stores = [copies.start(norm, norm_out), copies.start(state_two, state_out)]
    for store in stores:
        store.wait()


def edge_rows(cells, mate, cross, one, two, state_one, gain):
    columns, channels = cells.shape[1:]
    row = (columns, channels)
    padded = (columns + 16, channels)
    packed = ((12 * channels, 2 * channels), jnp.bfloat16)
    operands = (cells, mate, cross, one, two, state_one, gain)
    return pl.pallas_call(
        edge_body,
        in_specs=[anywhere] + [in_vmem] * 2 + [anywhere] * 4,
        out_specs=[anywhere] * 2,
        out_shape=[
            jax.ShapeDtypeStruct((4, *row), jnp.float32),
            jax.ShapeDtypeStruct((4, *row), jnp.bfloat16),
        ],
        scratch_shapes=[
            *scratch(((4, *row), jnp.float32), *[(a.shape, a.dtype) for a in operands[3:]]),
            *scratch(
                packed,
                packed,
                ((4, *row), jnp.float32),
                ((4, *row), jnp.bfloat16),
                ((8, *padded), jnp.float32),
                ((8, *padded), jnp.float32),
            ),
            pltpu.SemaphoreType.DMA((8,)),
        ],
        compiler_params=pltpu.CompilerParams(vmem_limit_bytes=edge_vmem_bytes),
        cost_estimate=no_cost,
        name="residual_edge",
    )(*operands)


def band_place():
    band = lax.axis_index("band")
    return band == 0, band == lax.axis_size("band") - 1, lax.rem(band, 2) == 1


def blend(query, window, store):
    keys, channels = window.shape
    extended = jnp.concatenate([window, jnp.ones((keys, channels), jnp.bfloat16)], axis=1)
    columns = query.shape[0]
    block = 128 if columns % 128 == 0 else columns
    for start in range(0, columns, block):
        scores = lax.dot_general(
            query[pl.ds(start, block)],
            window,
            (((1,), (1,)), ((), ())),
            preferred_element_type=jnp.float32,
        )
        peak = jnp.max(scores, axis=-1, keepdims=True)
        lifted = jnp.exp2(scores - peak).astype(jnp.bfloat16)
        total = jnp.dot(lifted, extended, preferred_element_type=jnp.float32)
        store(pl.ds(start, block), total[:, :channels] / total[:, channels:])


def pick(chosen, candidates):
    picked = candidates[0]
    for i, candidate in enumerate(candidates[1:], 1):
        picked = jnp.where(chosen == i, candidate, picked)
    return picked


def key_offset(partners, low, far):
    view = lax.axis_index("view")
    first = jnp.bitwise_xor(partners[view, 0], view)
    second = jnp.bitwise_xor(partners[view, 1], view)
    return (jnp.maximum(first, second) if far else jnp.minimum(first, second)) - low


def band_row(edge, middle, r):
    inner = middle.shape[0]
    if r < 2:
        return edge.at[r]
    if r < inner + 2:
        return middle.at[r - 2]
    return edge.at[r - inner]


def picked_row(chosen, edges, middles, r):
    return pick(chosen, [band_row(e, m, r)[...] for e, m in zip(edges, middles)])


def finish(r, both, state, value_out, gain, result):
    message = jnp.dot(both[r], value_out[...], preferred_element_type=jnp.float32)
    result[r] = state[...] + scaled(message, gain[...])


def take(refs, *counts):
    groups = []
    for count in counts:
        groups.append(refs[:count])
        refs = refs[count:]
    return (*groups, refs)


def gather_keys(chosen, edges, middles, keys):
    for r in range(keys.shape[0]):
        keys[r] = pick(chosen, [band_row(e, m, r)[...] for e, m in zip(edges, middles)])


def attend_first_body(low, count, partners, *refs):
    middles, refs = take(refs, count)
    (
        edge, middle, query_weight, key_weight, tempers, query_edge, query_middle, out, keys
    ) = refs
    ask((edge, middle), query_weight, key_weight, tempers, query_edge, query_middle)
    columns, channels = out.shape[1:]
    chosen = key_offset(partners, low, False)
    for r in range(keys.shape[0]):
        keys[r] = pick(chosen, [m[r] for m in middles])
    for r in range(out.shape[0]):
        window = keys[r : r + 3].reshape(3 * columns, channels)

        def store(place, value, r=r):
            out[r, place] = value.astype(jnp.bfloat16)

        blend(query_middle.at[r + 1], window, store)


def attend_near_body(low, count, partners, *refs):
    edges, middles, refs = take(refs, count, count)
    query_edge, query_middle, out, keys = refs
    rows, columns, channels = keys.shape
    gather_keys(key_offset(partners, low, False), edges, middles, keys)
    for slot, r in enumerate((1, 2, rows - 3, rows - 2)):
        window = keys[r - 1 : r + 2].reshape(3 * columns, channels)

        def store(place, value, slot=slot):
            out[slot, place] = value.astype(jnp.bfloat16)

        blend(band_row(query_edge, query_middle, r), window, store)


def attend_far_body(low, count, partners, *refs):
    edges, middles, refs = take(refs, count, count)
    (
        query_edge, query_middle, near, first, state_edge, state_middle, value_out, gain,
        out, keys, both,
    ) = refs
    rows, columns, channels = keys.shape
    gather_keys(key_offset(partners, low, True), edges, middles, keys)
    for r in range(1, rows - 1):
        window = keys[r - 1 : r + 2].reshape(3 * columns, channels)
        other = band_row(near, first, r - 1)

        def store(place, value, r=r, other=other):
            both[r - 1, place] = (value + other[place].astype(jnp.float32)).astype(jnp.bfloat16)

        blend(band_row(query_edge, query_middle, r), window, store)
    for r in range(1, rows - 1):
        finish(r - 1, both, band_row(state_edge, state_middle, r), value_out, gain, out)


def end_windows(chosen, edges, above, below, keys):
    keys[0] = above
    keys[5] = below
    for r in range(4):
        keys[1 + r] = pick(chosen, [e[r] for e in edges])


def attend_ends_body(low, count, partners, *refs):
    edges, refs = take(refs, count)
    mate, cross, query_edge, out = refs[:4]
    outs, keys = refs[4:-1], refs[-1]
    columns, channels = out.shape[1:]
    first_band, last_band, odd = band_place()
    for i in range(mate.shape[0]):
        above = jnp.where(odd, mate[i], cross[i])
        below = jnp.where(odd, cross[i], mate[i])
        outs[2 * i][0] = jnp.where(first_band, jnp.zeros_like(above), above)
        outs[2 * i + 1][0] = jnp.where(last_band, jnp.zeros_like(below), below)
    chosen = key_offset(partners, low, False)
    above = pick(chosen, [a[0] for a in outs[0::2]])
    below = pick(chosen, [b[0] for b in outs[1::2]])
    end_windows(chosen, edges, above, below, keys)
    for end in range(2):
        window = keys[3 * end : 3 * end + 3].reshape(3 * columns, channels)

        def store(place, value, end=end):
            out[end, place] = value.astype(jnp.bfloat16)

        blend(query_edge.at[3 * end], window, store)


def attend_outer_body(low, count, partners, *refs):
    edges, aboves, belows, refs = take(refs, count, count, count)
    query_edge, ends, state_edge, value_out, gain, inner, out, keys, both, result, sems = refs
    rows, columns, channels = out.shape
    copies = Copies(sems)
    stores = [copies.start(inner, out.at[pl.ds(1, rows - 2)])]
    chosen = key_offset(partners, low, True)
    above = pick(chosen, [a[0] for a in aboves])
    below = pick(chosen, [b[0] for b in belows])
    end_windows(chosen, edges, above, below, keys)
    for end in range(2):
        window = keys[3 * end : 3 * end + 3].reshape(3 * columns, channels)

        def store(place, value, end=end):
            both[end, place] = (value + ends[end, place].astype(jnp.float32)).astype(jnp.bfloat16)

        blend(query_edge.at[3 * end], window, store)
    for end in range(2):
        finish(end, both, state_edge.at[3 * end], value_out, gain, result)
    stores += [copies.start(result.at[0], out.at[0]), copies.start(result.at[1], out.at[rows - 1])]
    for store in stores:
        store.wait()


def attend_first(partners, low, middles, edge, middle, query_weight, key_weight, tempers):
    rows, columns = tempers.shape
    channels = edge.shape[-1]
    operands = [*middles, edge, middle, query_weight, key_weight, tempers]
    like = jax.ShapeDtypeStruct
    return pl.pallas_call(
        functools.partial(attend_first_body, low, len(middles)),
        in_specs=[in_smem] + [in_vmem] * len(operands),
        out_specs=[in_vmem] * 3,
        out_shape=[
            like(edge.shape, jnp.bfloat16),
            like(middle.shape, jnp.bfloat16),
            like((rows - 6, columns, channels), jnp.bfloat16),
        ],
        scratch_shapes=[pltpu.VMEM(middle.shape, jnp.bfloat16)],
        compiler_params=pltpu.CompilerParams(vmem_limit_bytes=vmem_bytes),
        cost_estimate=no_cost,
        name="attend_first",
    )(partners, *operands)


def attend_near(partners, low, candidates, queries):
    rows = candidates[0][0].shape[0] + candidates[1][0].shape[0]
    columns, channels = queries[0].shape[1:]
    operands = [a for group in candidates for a in group] + list(queries)
    return pl.pallas_call(
        functools.partial(attend_near_body, low, len(candidates[0])),
        in_specs=[in_smem] + [in_vmem] * len(operands),
        out_specs=in_vmem,
        out_shape=jax.ShapeDtypeStruct((4, columns, channels), jnp.bfloat16),
        scratch_shapes=[pltpu.VMEM((rows, columns, channels), jnp.bfloat16)],
        compiler_params=pltpu.CompilerParams(vmem_limit_bytes=vmem_bytes),
        cost_estimate=no_cost,
        name="attend_near",
    )(partners, *operands)


def attend_far(partners, low, candidates, queries, near, first, states, value_out, gain):
    columns, channels = near.shape[1:]
    rows = near.shape[0] + first.shape[0]
    operands = [a for group in candidates for a in group]
    operands += [*queries, near, first, *states, value_out, gain]
    return pl.pallas_call(
        functools.partial(attend_far_body, low, len(candidates[0])),
        in_specs=[in_smem] + [in_vmem] * len(operands),
        out_specs=in_vmem,
        out_shape=jax.ShapeDtypeStruct((rows, columns, channels), jnp.float32),
        scratch_shapes=[
            pltpu.VMEM((rows + 2, columns, channels), jnp.bfloat16),
            pltpu.VMEM((rows, columns, channels), jnp.bfloat16),
        ],
        compiler_params=pltpu.CompilerParams(vmem_limit_bytes=vmem_bytes),
        cost_estimate=no_cost,
        name="attend_far",
    )(partners, *operands)


def attend_ends(partners, low, edges, mate, cross, query):
    columns, channels = query.shape[1:]
    row = jax.ShapeDtypeStruct((1, columns, channels), jnp.bfloat16)
    operands = [*edges, mate, cross, query]
    return pl.pallas_call(
        functools.partial(attend_ends_body, low, len(edges)),
        in_specs=[in_smem] + [in_vmem] * len(operands),
        out_specs=[in_vmem] * (1 + 2 * mate.shape[0]),
        out_shape=[jax.ShapeDtypeStruct((2, columns, channels), jnp.bfloat16)]
        + [row] * (2 * mate.shape[0]),
        scratch_shapes=[pltpu.VMEM((6, columns, channels), jnp.bfloat16)],
        compiler_params=pltpu.CompilerParams(vmem_limit_bytes=vmem_bytes),
        cost_estimate=no_cost,
        name="attend_ends",
    )(partners, *operands)


def attend_outer(partners, low, sides, query, ends, state, value_out, gain, inner):
    rows, columns, channels = inner.shape
    operands = [a for group in sides for a in group]
    operands += [query, ends, state, value_out, gain, inner]
    return pl.pallas_call(
        functools.partial(attend_outer_body, low, len(sides[0])),
        in_specs=[in_smem] + [in_vmem] * len(operands),
        out_specs=anywhere,
        out_shape=jax.ShapeDtypeStruct((rows + 2, columns, channels), jnp.float32),
        scratch_shapes=[
            pltpu.VMEM((6, columns, channels), jnp.bfloat16),
            pltpu.VMEM((2, columns, channels), jnp.bfloat16),
            pltpu.VMEM((2, columns, channels), jnp.float32),
            pltpu.SemaphoreType.DMA((3,)),
        ],
        compiler_params=pltpu.CompilerParams(vmem_limit_bytes=vmem_bytes),
        cost_estimate=no_cost,
        name="attend_outer",
    )(partners, *operands)


def edge_halos_body(*refs):
    edges, (mate, cross) = refs[:-2], refs[-2:]
    odd = band_place()[2]
    for i, edge in enumerate(edges):
        mate[i] = jnp.where(odd, edge[0], edge[3])
        cross[i] = jnp.where(odd, edge[3], edge[0])


def edge_halos(edges):
    rows = jax.ShapeDtypeStruct((len(edges), *edges[0].shape[1:]), jnp.bfloat16)
    return pl.pallas_call(
        edge_halos_body,
        in_specs=[in_vmem] * len(edges),
        out_specs=[in_vmem] * 2,
        out_shape=[rows, rows],
        compiler_params=pltpu.CompilerParams(vmem_limit_bytes=vmem_bytes),
        cost_estimate=no_cost,
        name="edge_halos",
    )(*edges)


def swap(cells, views, offset):
    return lax.ppermute(cells, "view", [(i, i ^ offset) for i in range(views)])


def gather_direct(cells, views):
    return {1 << i: swap(cells, views, 1 << i) for i in range((views - 1).bit_length())}


def relay(held, views, by_low):
    for offset in range(1, views):
        bit = offset & -offset if by_low else 1 << (offset.bit_length() - 1)
        if bit != offset:
            held[offset] = swap(held[offset ^ bit], views, bit)


def swap_bands(mate, cross, bands):
    mates = [(i, i ^ 1) for i in range(bands)]
    crosses = [(i, i + 1) for i in range(1, bands - 1, 2)]
    crosses = crosses + [(j, i) for i, j in crosses]
    return lax.ppermute(mate, "band", mates), lax.ppermute(cross, "band", crosses)


def per_device(
    features, tempers, partners, conv_one, conv_two, query_weight, key_weight,
    value_weight, out_weight, norm_gain, message_gain,
):
    views = lax.axis_size("view")
    bands = lax.axis_size("band")
    cells, temper, gain = features[0], tempers[0], norm_gain[None]

    state_one, state_middle, middle = middle_rows(cells, conv_one, conv_two, gain)
    middles = gather_direct(middle, views)
    halo_cells, middle = lax.optimization_barrier((cells, middle))
    head, tail = halo_cells[:2].astype(jnp.bfloat16), halo_cells[-2:].astype(jnp.bfloat16)
    odd = band_place()[2]
    mate, cross = swap_bands(jnp.where(odd, head, tail), jnp.where(odd, tail, head), bands)
    state_edge, edge = edge_rows(cells, mate, cross, conv_one, conv_two, state_one, gain)
    edges = gather_direct(edge, views)

    def candidates(groups, low, high):
        return [[group[i] for i in range(low, high + 1)] for group in groups]

    near_ends, far_ends = (1, max(1, views - 2)), (min(2, views - 1), views - 1)
    direct = list(edges)
    *queries, first = attend_first(
        partners, 1, [middles[i] for i in direct], edge, middle, query_weight, key_weight, temper
    )
    value_out = jnp.dot(value_weight, out_weight, preferred_element_type=jnp.float32).astype(
        jnp.bfloat16
    )
    edges, middles, queries, first, value_out = lax.optimization_barrier(
        (edges, middles, queries, first, value_out)
    )
    mate, cross = swap_bands(*edge_halos([edges[i] for i in direct]), bands)
    relay(edges, views, False)
    relay(middles, views, True)
    near = attend_near(partners, near_ends[0], candidates((edges, middles), *near_ends), queries)
    mate, cross, near = lax.optimization_barrier((mate, cross, near))
    near_edges = candidates((edges,), *near_ends)[0]
    ends, *halos = attend_ends(partners, near_ends[0], near_edges, mate, cross, queries[0])
    edges, middles, halos, ends = lax.optimization_barrier((edges, middles, halos, ends))
    above = dict(zip(direct, halos[0::2]))
    below = dict(zip(direct, halos[1::2]))
    relay(above, views, True)
    relay(below, views, False)
    rest = (value_out, message_gain[None])
    inner = attend_far(
        partners, far_ends[0], candidates((edges, middles), *far_ends), queries, near, first,
        (state_edge, state_middle), *rest,
    )
    refined = attend_outer(
        partners, far_ends[0], candidates((edges, above, below), *far_ends), queries[0], ends,
        state_edge, *rest, inner,
    )
    return refined[None]


def solution(mesh):
    whole = P()
    in_specs = (P("view", "band", None, None), P("view", "band", None)) + (whole,) * 9
    return jax.shard_map(
        per_device, mesh=mesh, in_specs=in_specs,
        out_specs=P("view", "band", None, None), check_vma=False,
    )
```

```python
import functools
import math

import jax
import jax.numpy as jnp
from jax import lax
from jax.experimental import pallas as pl
from jax.experimental.pallas import tpu as pltpu
from jax.sharding import PartitionSpec as P

epsilon = 1e-06
vmem_bytes = 28 * 1024 * 1024
edge_vmem_bytes = 50 * 1024 * 1024
whole_vmem_bytes = 56 * 1024 * 1024
in_vmem = pl.BlockSpec(memory_space=pltpu.VMEM)
in_smem = pl.BlockSpec(memory_space=pltpu.SMEM)
no_cost = pl.CostEstimate(flops=0, bytes_accessed=0, transcendentals=0)
anywhere = pl.BlockSpec(memory_space=pl.ANY)


def silu(v):
    half = 0.5 * v
    return half * jnp.tanh(half) + half


def scaled(values, gain):
    mean_square = jnp.mean(values * values, axis=-1, keepdims=True)
    return values * lax.rsqrt(mean_square + epsilon) * gain


class Copies:
    def __init__(self, semaphores):
        self.semaphores = semaphores
        self.count = 0

    def start(self, source, target):
        copy = pltpu.make_async_copy(source, target, self.semaphores.at[self.count])
        self.count += 1
        copy.start()
        return copy

    def start_one(self, sources, chosen, target):
        slot = self.semaphores.at[self.count]
        self.count += 1
        for i, source in enumerate(sources):

            @pl.when(chosen == i)
            def _(source=source):
                pltpu.make_async_copy(source, target, slot).start()

        return pltpu.make_async_copy(sources[0], target, slot)


def clear(pad):
    slots, length, channels = pad.shape
    zeros = jnp.zeros((8, channels), jnp.float32)
    for slot in range(slots):
        pad[slot, 0:8] = zeros
        pad[slot, length - 8 : length] = zeros


def place(value, pad, slot):
    pad[slot, 8 : 8 + value.shape[0]] = value


def pack(kernel, out):
    channels = kernel.shape[2]
    zero = jnp.zeros((channels, channels), jnp.bfloat16)
    for j in range(4):
        for b in range(3):
            rows = pl.ds((3 * j + b) * channels, channels)
            out[rows, :channels] = kernel[j, b] if j < 3 else zero
            out[rows, channels:] = kernel[j - 1, b] if j > 0 else zero


def row_pair(pad, first, weights):
    columns = pad.shape[1] - 16
    block = 128 if columns % 128 == 0 else columns
    outs = []
    for start in range(7, 7 + columns, block):
        lhs = [pad[first + j, start + b : start + b + block] for j in range(4) for b in range(3)]
        lhs = jnp.concatenate(lhs, axis=-1).astype(jnp.bfloat16)
        outs.append(jnp.dot(lhs, weights[...], preferred_element_type=jnp.float32))
    return jnp.concatenate(outs, axis=0)


def ask(norm, query_weight, key_weight, tempers, query_edge, query_middle):
    rows, channels = tempers.shape[0], norm[0].shape[-1]
    mixing = lax.dot_general(
        query_weight[...],
        key_weight[...],
        (((1,), (1,)), ((), ())),
        preferred_element_type=jnp.float32,
    ).astype(jnp.bfloat16)
    scales = tempers[...].T * (math.log2(math.e) / math.sqrt(channels))
    for r in range(rows):
        row = band_row(*norm, r)[...]
        mixed = jnp.dot(row, mixing, preferred_element_type=jnp.float32)
        query = (mixed * scales[:, r : r + 1]).astype(jnp.bfloat16)
        band_row(query_edge, query_middle, r)[...] = query


def middle_body(
    cells, one, two, gain, mate_out, cross_out, state_one_out, state_out, norm_out,
    held, one_held, two_held, gain_held, mate, cross, w1, w2, state_one, state_two, norm, x1, x2,
    sems,
):
    rows = cells.shape[0]
    channels = cells.shape[2]
    copies = Copies(sems)
    kernels = [copies.start(one, one_held), copies.start(two, two_held)]
    loads = [copies.start(cells.at[r], held.at[r]) for r in range(4)]
    later = [copies.start(cells.at[r], held.at[r]) for r in range(4, rows)]
    later.append(copies.start(gain, gain_held))
    clear(x1)
    clear(x2)

    def convolve_one(first):
        out = row_pair(x1, first, w1)
        for o in range(2):
            r = first + 1 + o
            state = held[r] + out[:, o * channels : (o + 1) * channels]
            state_one[r - 1] = state
            place(silu(state), x2, r - 1)

    def convolve_two(first):
        out = row_pair(x2, first, w2)
        for o in range(2):
            slot = first + o
            state = state_one[slot + 1] + out[:, o * channels : (o + 1) * channels]
            state_two[slot] = state
            norm[slot] = scaled(state, gain_held[...]).astype(jnp.bfloat16)

    for load in kernels:
        load.wait()
    pack(one_held, w1)
    pack(two_held, w2)
    for load in loads:
        load.wait()
    for r in range(4):
        place(silu(held[r]), x1, r)
    for load in later:
        load.wait()
    odd = band_place()[2]
    for r in range(2):
        head, tail = held[r].astype(jnp.bfloat16), held[rows - 2 + r].astype(jnp.bfloat16)
        mate[r] = jnp.where(odd, head, tail)
        cross[r] = jnp.where(odd, tail, head)
    for first in range(0, rows - 2, 2):
        convolve_one(first)
        for r in range(first + 4, min(first + 6, rows)):
            place(silu(held[r]), x1, r)
        if 2 <= first < rows - 4:
            convolve_two(first - 2)
    stores = [
        copies.start(mate, mate_out),
        copies.start(cross, cross_out),
        copies.start(state_one.at[pl.ds(0, 2)], state_one_out.at[pl.ds(0, 2)]),
        copies.start(state_one.at[pl.ds(rows - 4, 2)], state_one_out.at[pl.ds(2, 2)]),
        copies.start(norm.at[pl.ds(0, rows - 6)], norm_out.at[pl.ds(0, rows - 6)]),
        copies.start(state_two.at[pl.ds(0, rows - 6)], state_out.at[pl.ds(0, rows - 6)]),
    ]
    convolve_two(rows - 6)
    last = pl.ds(rows - 6, 2)
    stores += [
        copies.start(norm.at[last], norm_out.at[last]),
        copies.start(state_two.at[last], state_out.at[last]),
    ]
    for store in stores:
        store.wait()


def scratch(*arrays):
    return [pltpu.VMEM(shape, kind) for shape, kind in arrays]


def middle_rows(cells, one, two, gain):
    rows, columns, channels = cells.shape
    row = (columns, channels)
    padded = (columns + 16, channels)
    packed = ((12 * channels, 2 * channels), jnp.bfloat16)
    operands = (cells, one, two, gain)
    return pl.pallas_call(
        middle_body,
        in_specs=[anywhere] * 4,
        out_specs=[anywhere] * 5,
        out_shape=[
            jax.ShapeDtypeStruct((2, *row), jnp.bfloat16),
            jax.ShapeDtypeStruct((2, *row), jnp.bfloat16),
            jax.ShapeDtypeStruct((4, *row), jnp.float32),
            jax.ShapeDtypeStruct((rows - 4, *row), jnp.float32),
            jax.ShapeDtypeStruct((rows - 4, *row), jnp.bfloat16),
        ],
        scratch_shapes=[
            *scratch(*[(a.shape, a.dtype) for a in operands]),
            *scratch(
                ((2, *row), jnp.bfloat16),
                ((2, *row), jnp.bfloat16),
                packed,
                packed,
                ((rows - 2, *row), jnp.float32),
                ((rows - 4, *row), jnp.float32),
                ((rows - 4, *row), jnp.bfloat16),
                ((rows, *padded), jnp.float32),
                ((rows - 2, *padded), jnp.float32),
            ),
            pltpu.SemaphoreType.DMA((rows + 11,)),
        ],
        compiler_params=pltpu.CompilerParams(vmem_limit_bytes=whole_vmem_bytes),
        cost_estimate=no_cost,
        name="residual_middle",
    )(*operands)


def edge_body(
    cells, mate, cross, one, two, state_one, gain, state_out, norm_out,
    held, one_held, two_held, state_held, gain_held, w1, w2, state_two, norm, x1, x2, sems,
):
    rows = cells.shape[0]
    channels = cells.shape[2]
    first_band, last_band, odd = band_place()
    copies = Copies(sems)
    loads = [
        copies.start(cells.at[pl.ds(0, 2)], held.at[pl.ds(0, 2)]),
        copies.start(cells.at[pl.ds(rows - 2, 2)], held.at[pl.ds(2, 2)]),
    ]
    later = [
        copies.start(one, one_held),
        copies.start(two, two_held),
        copies.start(state_one, state_held),
        copies.start(gain, gain_held),
    ]
    clear(x1)
    clear(x2)
    for load in loads:
        load.wait()
    for r in range(2):
        place(silu(held[r]), x1, 2 + r)
        place(silu(held[2 + r]), x1, 4 + r)
    outside = []
    for r in range(2):
        mate_row = mate[r].astype(jnp.float32)
        cross_row = cross[r].astype(jnp.float32)
        over = jnp.where(first_band, 0.0, jnp.where(odd, mate_row, cross_row))
        under = jnp.where(last_band, 0.0, jnp.where(odd, cross_row, mate_row))
        place(silu(over), x1, r)
        place(silu(under), x1, 6 + r)
        outside.append((over, under))
    over, under = outside[1][0], outside[0][1]
    for load in later:
        load.wait()
    pack(one_held, w1)
    pack(two_held, w2)
    out = row_pair(x1, 0, w1)
    over = over + out[:, :channels]
    top = held[0] + out[:, channels:]
    out = row_pair(x1, 4, w1)
    bottom = held[3] + out[:, :channels]
    under = under + out[:, channels:]
    for r in range(2):
        place(silu(state_held[r]), x2, 2 + r)
        place(silu(state_held[2 + r]), x2, 4 + r)
    place(jnp.where(first_band, 0.0, silu(over)), x2, 0)
    place(silu(top), x2, 1)
    place(silu(bottom), x2, 6)
    place(jnp.where(last_band, 0.0, silu(under)), x2, 7)
    for slot, states in ((0, (top, state_held[0])), (2, (state_held[3], bottom))):
        out = row_pair(x2, 2 * slot, w2)
        for o in range(2):
            state = states[o] + out[:, o * channels : (o + 1) * channels]
            state_two[slot + o] = state
            norm[slot + o] = scaled(state, gain_held[...]).astype(jnp.bfloat16)
    stores = [copies.start(norm, norm_out), copies.start(state_two, state_out)]
    for store in stores:
        store.wait()


def edge_rows(cells, mate, cross, one, two, state_one, gain):
    columns, channels = cells.shape[1:]
    row = (columns, channels)
    padded = (columns + 16, channels)
    packed = ((12 * channels, 2 * channels), jnp.bfloat16)
    operands = (cells, mate, cross, one, two, state_one, gain)
    return pl.pallas_call(
        edge_body,
        in_specs=[anywhere] + [in_vmem] * 2 + [anywhere] * 4,
        out_specs=[anywhere] * 2,
        out_shape=[
            jax.ShapeDtypeStruct((4, *row), jnp.float32),
            jax.ShapeDtypeStruct((4, *row), jnp.bfloat16),
        ],
        scratch_shapes=[
            *scratch(((4, *row), jnp.float32), *[(a.shape, a.dtype) for a in operands[3:]]),
            *scratch(
                packed,
                packed,
                ((4, *row), jnp.float32),
                ((4, *row), jnp.bfloat16),
                ((8, *padded), jnp.float32),
                ((8, *padded), jnp.float32),
            ),
            pltpu.SemaphoreType.DMA((8,)),
        ],
        compiler_params=pltpu.CompilerParams(vmem_limit_bytes=edge_vmem_bytes),
        cost_estimate=no_cost,
        name="residual_edge",
    )(*operands)


def band_place():
    band = lax.axis_index("band")
    return band == 0, band == lax.axis_size("band") - 1, lax.rem(band, 2) == 1


def blend(query, window, store):
    keys, channels = window.shape
    extended = jnp.concatenate([window, jnp.ones((keys, channels), jnp.bfloat16)], axis=1)
    columns = query.shape[0]
    block = 128 if columns % 128 == 0 else columns
    for start in range(0, columns, block):
        scores = lax.dot_general(
            query[pl.ds(start, block)],
            window,
            (((1,), (1,)), ((), ())),
            preferred_element_type=jnp.float32,
        )
        peak = jnp.max(scores, axis=-1, keepdims=True)
        lifted = jnp.exp2(scores - peak).astype(jnp.bfloat16)
        total = jnp.dot(lifted, extended, preferred_element_type=jnp.float32)
        store(pl.ds(start, block), total[:, :channels] / total[:, channels:])


def pick(chosen, candidates):
    picked = candidates[0]
    for i, candidate in enumerate(candidates[1:], 1):
        picked = jnp.where(chosen == i, candidate, picked)
    return picked


def key_offset(partners, low, far):
    view = lax.axis_index("view")
    first = jnp.bitwise_xor(partners[view, 0], view)
    second = jnp.bitwise_xor(partners[view, 1], view)
    return (jnp.maximum(first, second) if far else jnp.minimum(first, second)) - low


def band_row(edge, middle, r):
    inner = middle.shape[0]
    if r < 2:
        return edge.at[r]
    if r < inner + 2:
        return middle.at[r - 2]
    return edge.at[r - inner]


def picked_row(chosen, edges, middles, r):
    return pick(chosen, [band_row(e, m, r)[...] for e, m in zip(edges, middles)])


def finish(r, both, state, value_out, gain, result):
    message = jnp.dot(both[r], value_out[...], preferred_element_type=jnp.float32)
    result[r] = state[...] + scaled(message, gain[...])


def take(refs, *counts):
    groups = []
    for count in counts:
        groups.append(refs[:count])
        refs = refs[count:]
    return (*groups, refs)


def gather_keys(chosen, edges, middles, keys):
    for r in range(keys.shape[0]):
        keys[r] = pick(chosen, [band_row(e, m, r)[...] for e, m in zip(edges, middles)])


def attend_first_body(low, count, partners, *refs):
    middles, refs = take(refs, count)
    (
        edge, middle, query_weight, key_weight, tempers, query_edge, query_middle, out, keys
    ) = refs
    ask((edge, middle), query_weight, key_weight, tempers, query_edge, query_middle)
    columns, channels = out.shape[1:]
    chosen = key_offset(partners, low, False)
    for r in range(keys.shape[0]):
        keys[r] = pick(chosen, [m[r] for m in middles])
    for r in range(out.shape[0]):
        window = keys[r : r + 3].reshape(3 * columns, channels)

        def store(place, value, r=r):
            out[r, place] = value.astype(jnp.bfloat16)

        blend(query_middle.at[r + 1], window, store)


def attend_near_body(low, count, partners, *refs):
    edges, middles, refs = take(refs, count, count)
    query_edge, query_middle, out, keys = refs
    rows, columns, channels = keys.shape
    gather_keys(key_offset(partners, low, False), edges, middles, keys)
    for slot, r in enumerate((1, 2, rows - 3, rows - 2)):
        window = keys[r - 1 : r + 2].reshape(3 * columns, channels)

        def store(place, value, slot=slot):
            out[slot, place] = value.astype(jnp.bfloat16)

        blend(band_row(query_edge, query_middle, r), window, store)


def attend_far_body(low, count, partners, *refs):
    edges, middles, refs = take(refs, count, count)
    (
        query_edge, query_middle, near, first, state_edge, state_middle, value_out, gain,
        out, keys, both,
    ) = refs
    rows, columns, channels = keys.shape
    gather_keys(key_offset(partners, low, True), edges, middles, keys)
    for r in range(1, rows - 1):
        window = keys[r - 1 : r + 2].reshape(3 * columns, channels)
        other = band_row(near, first, r - 1)

        def store(place, value, r=r, other=other):
            both[r - 1, place] = (value + other[place].astype(jnp.float32)).astype(jnp.bfloat16)

        blend(band_row(query_edge, query_middle, r), window, store)
    for r in range(1, rows - 1):
        finish(r - 1, both, band_row(state_edge, state_middle, r), value_out, gain, out)


def end_windows(chosen, edges, above, below, keys):
    keys[0] = above
    keys[5] = below
    for r in range(4):
        keys[1 + r] = pick(chosen, [e[r] for e in edges])


def attend_ends_body(low, count, partners, *refs):
    edges, refs = take(refs, count)
    mate, cross, query_edge, out = refs[:4]
    outs, keys = refs[4:-1], refs[-1]
    columns, channels = out.shape[1:]
    first_band, last_band, odd = band_place()
    for i in range(mate.shape[0]):
        above = jnp.where(odd, mate[i], cross[i])
        below = jnp.where(odd, cross[i], mate[i])
        outs[2 * i][0] = jnp.where(first_band, jnp.zeros_like(above), above)
        outs[2 * i + 1][0] = jnp.where(last_band, jnp.zeros_like(below), below)
    chosen = key_offset(partners, low, False)
    above = pick(chosen, [a[0] for a in outs[0::2]])
    below = pick(chosen, [b[0] for b in outs[1::2]])
    end_windows(chosen, edges, above, below, keys)
    for end in range(2):
        window = keys[3 * end : 3 * end + 3].reshape(3 * columns, channels)

        def store(place, value, end=end):
            out[end, place] = value.astype(jnp.bfloat16)

        blend(query_edge.at[3 * end], window, store)


def attend_outer_body(low, count, partners, *refs):
    edges, aboves, belows, refs = take(refs, count, count, count)
    query_edge, ends, state_edge, value_out, gain, inner, out, keys, both, result, sems = refs
    rows, columns, channels = out.shape
    copies = Copies(sems)
    stores = [copies.start(inner, out.at[pl.ds(1, rows - 2)])]
    chosen = key_offset(partners, low, True)
    above = pick(chosen, [a[0] for a in aboves])
    below = pick(chosen, [b[0] for b in belows])
    end_windows(chosen, edges, above, below, keys)
    for end in range(2):
        window = keys[3 * end : 3 * end + 3].reshape(3 * columns, channels)

        def store(place, value, end=end):
            both[end, place] = (value + ends[end, place].astype(jnp.float32)).astype(jnp.bfloat16)

        blend(query_edge.at[3 * end], window, store)
    for end in range(2):
        finish(end, both, state_edge.at[3 * end], value_out, gain, result)
    stores += [copies.start(result.at[0], out.at[0]), copies.start(result.at[1], out.at[rows - 1])]
    for store in stores:
        store.wait()


def attend_first(partners, low, middles, edge, middle, query_weight, key_weight, tempers):
    rows, columns = tempers.shape
    channels = edge.shape[-1]
    operands = [*middles, edge, middle, query_weight, key_weight, tempers]
    like = jax.ShapeDtypeStruct
    return pl.pallas_call(
        functools.partial(attend_first_body, low, len(middles)),
        in_specs=[in_smem] + [in_vmem] * len(operands),
        out_specs=[in_vmem] * 3,
        out_shape=[
            like(edge.shape, jnp.bfloat16),
            like(middle.shape, jnp.bfloat16),
            like((rows - 6, columns, channels), jnp.bfloat16),
        ],
        scratch_shapes=[pltpu.VMEM(middle.shape, jnp.bfloat16)],
        compiler_params=pltpu.CompilerParams(vmem_limit_bytes=vmem_bytes),
        cost_estimate=no_cost,
        name="attend_first",
    )(partners, *operands)


def attend_near(partners, low, candidates, queries):
    rows = candidates[0][0].shape[0] + candidates[1][0].shape[0]
    columns, channels = queries[0].shape[1:]
    operands = [a for group in candidates for a in group] + list(queries)
    return pl.pallas_call(
        functools.partial(attend_near_body, low, len(candidates[0])),
        in_specs=[in_smem] + [in_vmem] * len(operands),
        out_specs=in_vmem,
        out_shape=jax.ShapeDtypeStruct((4, columns, channels), jnp.bfloat16),
        scratch_shapes=[pltpu.VMEM((rows, columns, channels), jnp.bfloat16)],
        compiler_params=pltpu.CompilerParams(vmem_limit_bytes=vmem_bytes),
        cost_estimate=no_cost,
        name="attend_near",
    )(partners, *operands)


def attend_far(partners, low, candidates, queries, near, first, states, value_out, gain):
    columns, channels = near.shape[1:]
    rows = near.shape[0] + first.shape[0]
    operands = [a for group in candidates for a in group]
    operands += [*queries, near, first, *states, value_out, gain]
    return pl.pallas_call(
        functools.partial(attend_far_body, low, len(candidates[0])),
        in_specs=[in_smem] + [in_vmem] * len(operands),
        out_specs=in_vmem,
        out_shape=jax.ShapeDtypeStruct((rows, columns, channels), jnp.float32),
        scratch_shapes=[
            pltpu.VMEM((rows + 2, columns, channels), jnp.bfloat16),
            pltpu.VMEM((rows, columns, channels), jnp.bfloat16),
        ],
        compiler_params=pltpu.CompilerParams(vmem_limit_bytes=vmem_bytes),
        cost_estimate=no_cost,
        name="attend_far",
    )(partners, *operands)


def attend_ends(partners, low, edges, mate, cross, query):
    columns, channels = query.shape[1:]
    row = jax.ShapeDtypeStruct((1, columns, channels), jnp.bfloat16)
    operands = [*edges, mate, cross, query]
    return pl.pallas_call(
        functools.partial(attend_ends_body, low, len(edges)),
        in_specs=[in_smem] + [in_vmem] * len(operands),
        out_specs=[in_vmem] * (1 + 2 * mate.shape[0]),
        out_shape=[jax.ShapeDtypeStruct((2, columns, channels), jnp.bfloat16)]
        + [row] * (2 * mate.shape[0]),
        scratch_shapes=[pltpu.VMEM((6, columns, channels), jnp.bfloat16)],
        compiler_params=pltpu.CompilerParams(vmem_limit_bytes=vmem_bytes),
        cost_estimate=no_cost,
        name="attend_ends",
    )(partners, *operands)


def attend_outer(partners, low, sides, query, ends, state, value_out, gain, inner):
    rows, columns, channels = inner.shape
    operands = [a for group in sides for a in group]
    operands += [query, ends, state, value_out, gain, inner]
    return pl.pallas_call(
        functools.partial(attend_outer_body, low, len(sides[0])),
        in_specs=[in_smem] + [in_vmem] * len(operands),
        out_specs=anywhere,
        out_shape=jax.ShapeDtypeStruct((rows + 2, columns, channels), jnp.float32),
        scratch_shapes=[
            pltpu.VMEM((6, columns, channels), jnp.bfloat16),
            pltpu.VMEM((2, columns, channels), jnp.bfloat16),
            pltpu.VMEM((2, columns, channels), jnp.float32),
            pltpu.SemaphoreType.DMA((3,)),
        ],
        compiler_params=pltpu.CompilerParams(vmem_limit_bytes=vmem_bytes),
        cost_estimate=no_cost,
        name="attend_outer",
    )(partners, *operands)


def edge_halos_body(*refs):
    edges, (mate, cross) = refs[:-2], refs[-2:]
    odd = band_place()[2]
    for i, edge in enumerate(edges):
        mate[i] = jnp.where(odd, edge[0], edge[3])
        cross[i] = jnp.where(odd, edge[3], edge[0])


def edge_halos(edges):
    rows = jax.ShapeDtypeStruct((len(edges), *edges[0].shape[1:]), jnp.bfloat16)
    return pl.pallas_call(
        edge_halos_body,
        in_specs=[in_vmem] * len(edges),
        out_specs=[in_vmem] * 2,
        out_shape=[rows, rows],
        compiler_params=pltpu.CompilerParams(vmem_limit_bytes=vmem_bytes),
        cost_estimate=no_cost,
        name="edge_halos",
    )(*edges)


def swap(cells, views, offset):
    return lax.ppermute(cells, "view", [(i, i ^ offset) for i in range(views)])


def gather_direct(cells, views):
    return {1 << i: swap(cells, views, 1 << i) for i in range((views - 1).bit_length())}


def relay(held, views, by_low):
    for offset in range(1, views):
        bit = offset & -offset if by_low else 1 << (offset.bit_length() - 1)
        if bit != offset:
            held[offset] = swap(held[offset ^ bit], views, bit)


def swap_bands(mate, cross, bands):
    mates = [(i, i ^ 1) for i in range(bands)]
    crosses = [(i, i + 1) for i in range(1, bands - 1, 2)]
    crosses = crosses + [(j, i) for i, j in crosses]
    return lax.ppermute(mate, "band", mates), lax.ppermute(cross, "band", crosses)


def per_device(
    features, tempers, partners, conv_one, conv_two, query_weight, key_weight,
    value_weight, out_weight, norm_gain, message_gain,
):
    views = lax.axis_size("view")
    bands = lax.axis_size("band")
    cells, temper, gain = features[0], tempers[0], norm_gain[None]

    mate, cross, state_one, state_middle, middle = middle_rows(cells, conv_one, conv_two, gain)
    middles = gather_direct(middle, views)
    mate, cross = swap_bands(mate, cross, bands)
    state_edge, edge = edge_rows(cells, mate, cross, conv_one, conv_two, state_one, gain)
    edges = gather_direct(edge, views)

    def candidates(groups, low, high):
        return [[group[i] for i in range(low, high + 1)] for group in groups]

    near_ends, far_ends = (1, max(1, views - 2)), (min(2, views - 1), views - 1)
    direct = list(edges)
    *queries, first = attend_first(
        partners, 1, [middles[i] for i in direct], edge, middle, query_weight, key_weight, temper
    )
    value_out = jnp.dot(value_weight, out_weight, preferred_element_type=jnp.float32).astype(
        jnp.bfloat16
    )
    edges, middles, queries, first, value_out = lax.optimization_barrier(
        (edges, middles, queries, first, value_out)
    )
    mate, cross = swap_bands(*edge_halos([edges[i] for i in direct]), bands)
    relay(edges, views, False)
    relay(middles, views, True)
    near = attend_near(partners, near_ends[0], candidates((edges, middles), *near_ends), queries)
    mate, cross, near = lax.optimization_barrier((mate, cross, near))
    near_edges = candidates((edges,), *near_ends)[0]
    ends, *halos = attend_ends(partners, near_ends[0], near_edges, mate, cross, queries[0])
    edges, middles, halos, ends = lax.optimization_barrier((edges, middles, halos, ends))
    above = dict(zip(direct, halos[0::2]))
    below = dict(zip(direct, halos[1::2]))
    relay(above, views, True)
    relay(below, views, False)
    rest = (value_out, message_gain[None])
    inner = attend_far(
        partners, far_ends[0], candidates((edges, middles), *far_ends), queries, near, first,
        (state_edge, state_middle), *rest,
    )
    refined = attend_outer(
        partners, far_ends[0], candidates((edges, above, below), *far_ends), queries[0], ends,
        state_edge, *rest, inner,
    )
    return refined[None]


def solution(mesh):
    whole = P()
    in_specs = (P("view", "band", None, None), P("view", "band", None)) + (whole,) * 9
    return jax.shard_map(
        per_device, mesh=mesh, in_specs=in_specs,
        out_specs=P("view", "band", None, None), check_vma=False,
    )
```

```python
import functools
import math

import jax
import jax.numpy as jnp
from jax import lax
from jax.experimental import pallas as pl
from jax.experimental.pallas import tpu as pltpu
from jax.sharding import PartitionSpec as P

epsilon = 1e-06
vmem_bytes = 28 * 1024 * 1024
edge_vmem_bytes = 50 * 1024 * 1024
whole_vmem_bytes = 56 * 1024 * 1024
in_vmem = pl.BlockSpec(memory_space=pltpu.VMEM)
in_smem = pl.BlockSpec(memory_space=pltpu.SMEM)
no_cost = pl.CostEstimate(flops=0, bytes_accessed=0, transcendentals=0)
anywhere = pl.BlockSpec(memory_space=pl.ANY)


def silu(v):
    half = 0.5 * v
    return half * jnp.tanh(half) + half


def scaled(values, gain):
    mean_square = jnp.mean(values * values, axis=-1, keepdims=True)
    return values * lax.rsqrt(mean_square + epsilon) * gain


class Copies:
    def __init__(self, semaphores):
        self.semaphores = semaphores
        self.count = 0

    def start(self, source, target):
        copy = pltpu.make_async_copy(source, target, self.semaphores.at[self.count])
        self.count += 1
        copy.start()
        return copy

    def start_one(self, sources, chosen, target):
        slot = self.semaphores.at[self.count]
        self.count += 1
        for i, source in enumerate(sources):

            @pl.when(chosen == i)
            def _(source=source):
                pltpu.make_async_copy(source, target, slot).start()

        return pltpu.make_async_copy(sources[0], target, slot)


def clear(pad):
    slots, length, channels = pad.shape
    zeros = jnp.zeros((8, channels), jnp.float32)
    for slot in range(slots):
        pad[slot, 0:8] = zeros
        pad[slot, length - 8 : length] = zeros


def place(value, pad, slot):
    pad[slot, 8 : 8 + value.shape[0]] = value


def pack(kernel, out):
    channels = kernel.shape[2]
    zero = jnp.zeros((channels, channels), jnp.bfloat16)
    for j in range(4):
        for b in range(3):
            rows = pl.ds((3 * j + b) * channels, channels)
            out[rows, :channels] = kernel[j, b] if j < 3 else zero
            out[rows, channels:] = kernel[j - 1, b] if j > 0 else zero


def row_pair(pad, first, weights):
    columns = pad.shape[1] - 16
    block = 128 if columns % 128 == 0 else columns
    outs = []
    for start in range(7, 7 + columns, block):
        lhs = [pad[first + j, start + b : start + b + block] for j in range(4) for b in range(3)]
        lhs = jnp.concatenate(lhs, axis=-1).astype(jnp.bfloat16)
        outs.append(jnp.dot(lhs, weights[...], preferred_element_type=jnp.float32))
    return jnp.concatenate(outs, axis=0)


def ask(norm, query_weight, key_weight, tempers, query_edge, query_middle):
    rows, channels = tempers.shape[0], norm[0].shape[-1]
    mixing = lax.dot_general(
        query_weight[...],
        key_weight[...],
        (((1,), (1,)), ((), ())),
        preferred_element_type=jnp.float32,
    ).astype(jnp.bfloat16)
    scales = tempers[...].T * (math.log2(math.e) / math.sqrt(channels))
    for r in range(rows):
        row = band_row(*norm, r)[...]
        mixed = jnp.dot(row, mixing, preferred_element_type=jnp.float32)
        query = (mixed * scales[:, r : r + 1]).astype(jnp.bfloat16)
        band_row(query_edge, query_middle, r)[...] = query


def middle_body(
    cells, one, two, gain, mate_out, cross_out, state_one_out, state_out, norm_out,
    held, one_held, two_held, gain_held, mate, cross, w1, w2, state_one, state_two, norm, x1, x2,
    sems,
):
    rows = cells.shape[0]
    channels = cells.shape[2]
    copies = Copies(sems)
    kernels = [copies.start(one, one_held), copies.start(two, two_held)]
    loads = [copies.start(cells.at[r], held.at[r]) for r in range(4)]
    later = [copies.start(cells.at[r], held.at[r]) for r in range(4, rows)]
    later.append(copies.start(gain, gain_held))
    clear(x1)
    clear(x2)

    def convolve_one(first):
        out = row_pair(x1, first, w1)
        for o in range(2):
            r = first + 1 + o
            state = held[r] + out[:, o * channels : (o + 1) * channels]
            state_one[r - 1] = state
            place(silu(state), x2, r - 1)

    def convolve_two(first):
        out = row_pair(x2, first, w2)
        for o in range(2):
            slot = first + o
            state = state_one[slot + 1] + out[:, o * channels : (o + 1) * channels]
            state_two[slot] = state
            norm[slot] = scaled(state, gain_held[...]).astype(jnp.bfloat16)

    for load in kernels:
        load.wait()
    pack(one_held, w1)
    pack(two_held, w2)
    for load in loads:
        load.wait()
    for r in range(4):
        place(silu(held[r]), x1, r)
    for load in later:
        load.wait()
    odd = band_place()[2]
    for r in range(2):
        head, tail = held[r].astype(jnp.bfloat16), held[rows - 2 + r].astype(jnp.bfloat16)
        mate[r] = jnp.where(odd, head, tail)
        cross[r] = jnp.where(odd, tail, head)
    for first in range(0, rows - 2, 2):
        convolve_one(first)
        for r in range(first + 4, min(first + 6, rows)):
            place(silu(held[r]), x1, r)
    early = [
        copies.start(mate, mate_out),
        copies.start(cross, cross_out),
        copies.start(state_one.at[pl.ds(0, 2)], state_one_out.at[pl.ds(0, 2)]),
        copies.start(state_one.at[pl.ds(rows - 4, 2)], state_one_out.at[pl.ds(2, 2)]),
    ]
    for first in range(0, rows - 6, 2):
        convolve_two(first)
    stores = early + [
        copies.start(state_two.at[pl.ds(0, rows - 6)], state_out.at[pl.ds(0, rows - 6)]),
        copies.start(norm.at[pl.ds(0, rows - 6)], norm_out.at[pl.ds(0, rows - 6)]),
    ]
    convolve_two(rows - 6)
    last = pl.ds(rows - 6, 2)
    stores += [
        copies.start(norm.at[last], norm_out.at[last]),
        copies.start(state_two.at[last], state_out.at[last]),
    ]
    for store in stores:
        store.wait()


def scratch(*arrays):
    return [pltpu.VMEM(shape, kind) for shape, kind in arrays]


def middle_rows(cells, one, two, gain):
    rows, columns, channels = cells.shape
    row = (columns, channels)
    padded = (columns + 16, channels)
    packed = ((12 * channels, 2 * channels), jnp.bfloat16)
    operands = (cells, one, two, gain)
    return pl.pallas_call(
        middle_body,
        in_specs=[anywhere] * 4,
        out_specs=[anywhere] * 5,
        out_shape=[
            jax.ShapeDtypeStruct((2, *row), jnp.bfloat16),
            jax.ShapeDtypeStruct((2, *row), jnp.bfloat16),
            jax.ShapeDtypeStruct((4, *row), jnp.float32),
            jax.ShapeDtypeStruct((rows - 4, *row), jnp.float32),
            jax.ShapeDtypeStruct((rows - 4, *row), jnp.bfloat16),
        ],
        scratch_shapes=[
            *scratch(*[(a.shape, a.dtype) for a in operands]),
            *scratch(
                ((2, *row), jnp.bfloat16),
                ((2, *row), jnp.bfloat16),
                packed,
                packed,
                ((rows - 2, *row), jnp.float32),
                ((rows - 4, *row), jnp.float32),
                ((rows - 4, *row), jnp.bfloat16),
                ((rows, *padded), jnp.float32),
                ((rows - 2, *padded), jnp.float32),
            ),
            pltpu.SemaphoreType.DMA((rows + 11,)),
        ],
        compiler_params=pltpu.CompilerParams(vmem_limit_bytes=whole_vmem_bytes),
        cost_estimate=no_cost,
        name="residual_middle",
    )(*operands)


def edge_body(
    cells, mate, cross, one, two, state_one, gain, state_out, norm_out,
    held, one_held, two_held, state_held, gain_held, w1, w2, state_two, norm, x1, x2, sems,
):
    rows = cells.shape[0]
    channels = cells.shape[2]
    first_band, last_band, odd = band_place()
    copies = Copies(sems)
    loads = [
        copies.start(cells.at[pl.ds(0, 2)], held.at[pl.ds(0, 2)]),
        copies.start(cells.at[pl.ds(rows - 2, 2)], held.at[pl.ds(2, 2)]),
    ]
    later = [
        copies.start(one, one_held),
        copies.start(two, two_held),
        copies.start(state_one, state_held),
        copies.start(gain, gain_held),
    ]
    clear(x1)
    clear(x2)
    for load in loads:
        load.wait()
    for r in range(2):
        place(silu(held[r]), x1, 2 + r)
        place(silu(held[2 + r]), x1, 4 + r)
    outside = []
    for r in range(2):
        mate_row = mate[r].astype(jnp.float32)
        cross_row = cross[r].astype(jnp.float32)
        over = jnp.where(first_band, 0.0, jnp.where(odd, mate_row, cross_row))
        under = jnp.where(last_band, 0.0, jnp.where(odd, cross_row, mate_row))
        place(silu(over), x1, r)
        place(silu(under), x1, 6 + r)
        outside.append((over, under))
    over, under = outside[1][0], outside[0][1]
    for load in later:
        load.wait()
    pack(one_held, w1)
    pack(two_held, w2)
    out = row_pair(x1, 0, w1)
    over = over + out[:, :channels]
    top = held[0] + out[:, channels:]
    out = row_pair(x1, 4, w1)
    bottom = held[3] + out[:, :channels]
    under = under + out[:, channels:]
    for r in range(2):
        place(silu(state_held[r]), x2, 2 + r)
        place(silu(state_held[2 + r]), x2, 4 + r)
    place(jnp.where(first_band, 0.0, silu(over)), x2, 0)
    place(silu(top), x2, 1)
    place(silu(bottom), x2, 6)
    place(jnp.where(last_band, 0.0, silu(under)), x2, 7)
    for slot, states in ((0, (top, state_held[0])), (2, (state_held[3], bottom))):
        out = row_pair(x2, 2 * slot, w2)
        for o in range(2):
            state = states[o] + out[:, o * channels : (o + 1) * channels]
            state_two[slot + o] = state
            norm[slot + o] = scaled(state, gain_held[...]).astype(jnp.bfloat16)
    stores = [copies.start(norm, norm_out), copies.start(state_two, state_out)]
    for store in stores:
        store.wait()


def edge_rows(cells, mate, cross, one, two, state_one, gain):
    columns, channels = cells.shape[1:]
    row = (columns, channels)
    padded = (columns + 16, channels)
    packed = ((12 * channels, 2 * channels), jnp.bfloat16)
    operands = (cells, mate, cross, one, two, state_one, gain)
    return pl.pallas_call(
        edge_body,
        in_specs=[anywhere] + [in_vmem] * 2 + [anywhere] * 4,
        out_specs=[anywhere] * 2,
        out_shape=[
            jax.ShapeDtypeStruct((4, *row), jnp.float32),
            jax.ShapeDtypeStruct((4, *row), jnp.bfloat16),
        ],
        scratch_shapes=[
            *scratch(((4, *row), jnp.float32), *[(a.shape, a.dtype) for a in operands[3:]]),
            *scratch(
                packed,
                packed,
                ((4, *row), jnp.float32),
                ((4, *row), jnp.bfloat16),
                ((8, *padded), jnp.float32),
                ((8, *padded), jnp.float32),
            ),
            pltpu.SemaphoreType.DMA((8,)),
        ],
        compiler_params=pltpu.CompilerParams(vmem_limit_bytes=edge_vmem_bytes),
        cost_estimate=no_cost,
        name="residual_edge",
    )(*operands)


def band_place():
    band = lax.axis_index("band")
    return band == 0, band == lax.axis_size("band") - 1, lax.rem(band, 2) == 1


def blend(query, window, store):
    keys, channels = window.shape
    extended = jnp.concatenate([window, jnp.ones((keys, channels), jnp.bfloat16)], axis=1)
    columns = query.shape[0]
    block = 128 if columns % 128 == 0 else columns
    for start in range(0, columns, block):
        scores = lax.dot_general(
            query[pl.ds(start, block)],
            window,
            (((1,), (1,)), ((), ())),
            preferred_element_type=jnp.float32,
        )
        peak = jnp.max(scores, axis=-1, keepdims=True)
        lifted = jnp.exp2(scores - peak).astype(jnp.bfloat16)
        total = jnp.dot(lifted, extended, preferred_element_type=jnp.float32)
        store(pl.ds(start, block), total[:, :channels] / total[:, channels:])


def pick(chosen, candidates):
    picked = candidates[0]
    for i, candidate in enumerate(candidates[1:], 1):
        picked = jnp.where(chosen == i, candidate, picked)
    return picked


def key_offset(partners, low, far):
    view = lax.axis_index("view")
    first = jnp.bitwise_xor(partners[view, 0], view)
    second = jnp.bitwise_xor(partners[view, 1], view)
    return (jnp.maximum(first, second) if far else jnp.minimum(first, second)) - low


def band_row(edge, middle, r):
    inner = middle.shape[0]
    if r < 2:
        return edge.at[r]
    if r < inner + 2:
        return middle.at[r - 2]
    return edge.at[r - inner]


def picked_row(chosen, edges, middles, r):
    return pick(chosen, [band_row(e, m, r)[...] for e, m in zip(edges, middles)])


def finish(r, both, state, value_out, gain, result):
    message = jnp.dot(both[r], value_out[...], preferred_element_type=jnp.float32)
    result[r] = state[...] + scaled(message, gain[...])


def take(refs, *counts):
    groups = []
    for count in counts:
        groups.append(refs[:count])
        refs = refs[count:]
    return (*groups, refs)


def gather_keys(chosen, edges, middles, keys):
    for r in range(keys.shape[0]):
        keys[r] = pick(chosen, [band_row(e, m, r)[...] for e, m in zip(edges, middles)])


def attend_first_body(low, count, partners, *refs):
    middles, refs = take(refs, count)
    (
        edge, middle, query_weight, key_weight, tempers, query_edge, query_middle, out, keys
    ) = refs
    ask((edge, middle), query_weight, key_weight, tempers, query_edge, query_middle)
    columns, channels = out.shape[1:]
    chosen = key_offset(partners, low, False)
    for r in range(keys.shape[0]):
        keys[r] = pick(chosen, [m[r] for m in middles])
    for r in range(out.shape[0]):
        window = keys[r : r + 3].reshape(3 * columns, channels)

        def store(place, value, r=r):
            out[r, place] = value.astype(jnp.bfloat16)

        blend(query_middle.at[r + 1], window, store)


def attend_near_body(low, count, partners, *refs):
    edges, middles, refs = take(refs, count, count)
    query_edge, query_middle, out, keys = refs
    rows, columns, channels = keys.shape
    gather_keys(key_offset(partners, low, False), edges, middles, keys)
    for slot, r in enumerate((1, 2, rows - 3, rows - 2)):
        window = keys[r - 1 : r + 2].reshape(3 * columns, channels)

        def store(place, value, slot=slot):
            out[slot, place] = value.astype(jnp.bfloat16)

        blend(band_row(query_edge, query_middle, r), window, store)


def attend_far_body(low, count, partners, *refs):
    edges, middles, refs = take(refs, count, count)
    (
        query_edge, query_middle, near, first, state_edge, state_middle, value_out, gain,
        out, keys, both,
    ) = refs
    rows, columns, channels = keys.shape
    gather_keys(key_offset(partners, low, True), edges, middles, keys)
    for r in range(1, rows - 1):
        window = keys[r - 1 : r + 2].reshape(3 * columns, channels)
        other = band_row(near, first, r - 1)

        def store(place, value, r=r, other=other):
            both[r - 1, place] = (value + other[place].astype(jnp.float32)).astype(jnp.bfloat16)

        blend(band_row(query_edge, query_middle, r), window, store)
    for r in range(1, rows - 1):
        finish(r - 1, both, band_row(state_edge, state_middle, r), value_out, gain, out)


def end_windows(chosen, edges, above, below, keys):
    keys[0] = above
    keys[5] = below
    for r in range(4):
        keys[1 + r] = pick(chosen, [e[r] for e in edges])


def attend_ends_body(low, count, partners, *refs):
    edges, refs = take(refs, count)
    mate, cross, query_edge, out = refs[:4]
    outs, keys = refs[4:-1], refs[-1]
    columns, channels = out.shape[1:]
    first_band, last_band, odd = band_place()
    for i in range(mate.shape[0]):
        above = jnp.where(odd, mate[i], cross[i])
        below = jnp.where(odd, cross[i], mate[i])
        outs[2 * i][0] = jnp.where(first_band, jnp.zeros_like(above), above)
        outs[2 * i + 1][0] = jnp.where(last_band, jnp.zeros_like(below), below)
    chosen = key_offset(partners, low, False)
    above = pick(chosen, [a[0] for a in outs[0::2]])
    below = pick(chosen, [b[0] for b in outs[1::2]])
    end_windows(chosen, edges, above, below, keys)
    for end in range(2):
        window = keys[3 * end : 3 * end + 3].reshape(3 * columns, channels)

        def store(place, value, end=end):
            out[end, place] = value.astype(jnp.bfloat16)

        blend(query_edge.at[3 * end], window, store)


def attend_outer_body(low, count, partners, *refs):
    edges, aboves, belows, refs = take(refs, count, count, count)
    query_edge, ends, state_edge, value_out, gain, inner, out, keys, both, result, sems = refs
    rows, columns, channels = out.shape
    copies = Copies(sems)
    stores = [copies.start(inner, out.at[pl.ds(1, rows - 2)])]
    chosen = key_offset(partners, low, True)
    above = pick(chosen, [a[0] for a in aboves])
    below = pick(chosen, [b[0] for b in belows])
    end_windows(chosen, edges, above, below, keys)
    for end in range(2):
        window = keys[3 * end : 3 * end + 3].reshape(3 * columns, channels)

        def store(place, value, end=end):
            both[end, place] = (value + ends[end, place].astype(jnp.float32)).astype(jnp.bfloat16)

        blend(query_edge.at[3 * end], window, store)
    for end in range(2):
        finish(end, both, state_edge.at[3 * end], value_out, gain, result)
    stores += [copies.start(result.at[0], out.at[0]), copies.start(result.at[1], out.at[rows - 1])]
    for store in stores:
        store.wait()


def attend_first(partners, low, middles, edge, middle, query_weight, key_weight, tempers):
    rows, columns = tempers.shape
    channels = edge.shape[-1]
    operands = [*middles, edge, middle, query_weight, key_weight, tempers]
    like = jax.ShapeDtypeStruct
    return pl.pallas_call(
        functools.partial(attend_first_body, low, len(middles)),
        in_specs=[in_smem] + [in_vmem] * len(operands),
        out_specs=[in_vmem] * 3,
        out_shape=[
            like(edge.shape, jnp.bfloat16),
            like(middle.shape, jnp.bfloat16),
            like((rows - 6, columns, channels), jnp.bfloat16),
        ],
        scratch_shapes=[pltpu.VMEM(middle.shape, jnp.bfloat16)],
        compiler_params=pltpu.CompilerParams(vmem_limit_bytes=vmem_bytes),
        cost_estimate=no_cost,
        name="attend_first",
    )(partners, *operands)


def attend_near(partners, low, candidates, queries):
    rows = candidates[0][0].shape[0] + candidates[1][0].shape[0]
    columns, channels = queries[0].shape[1:]
    operands = [a for group in candidates for a in group] + list(queries)
    return pl.pallas_call(
        functools.partial(attend_near_body, low, len(candidates[0])),
        in_specs=[in_smem] + [in_vmem] * len(operands),
        out_specs=in_vmem,
        out_shape=jax.ShapeDtypeStruct((4, columns, channels), jnp.bfloat16),
        scratch_shapes=[pltpu.VMEM((rows, columns, channels), jnp.bfloat16)],
        compiler_params=pltpu.CompilerParams(vmem_limit_bytes=vmem_bytes),
        cost_estimate=no_cost,
        name="attend_near",
    )(partners, *operands)


def attend_far(partners, low, candidates, queries, near, first, states, value_out, gain):
    columns, channels = near.shape[1:]
    rows = near.shape[0] + first.shape[0]
    operands = [a for group in candidates for a in group]
    operands += [*queries, near, first, *states, value_out, gain]
    return pl.pallas_call(
        functools.partial(attend_far_body, low, len(candidates[0])),
        in_specs=[in_smem] + [in_vmem] * len(operands),
        out_specs=in_vmem,
        out_shape=jax.ShapeDtypeStruct((rows, columns, channels), jnp.float32),
        scratch_shapes=[
            pltpu.VMEM((rows + 2, columns, channels), jnp.bfloat16),
            pltpu.VMEM((rows, columns, channels), jnp.bfloat16),
        ],
        compiler_params=pltpu.CompilerParams(vmem_limit_bytes=vmem_bytes),
        cost_estimate=no_cost,
        name="attend_far",
    )(partners, *operands)


def attend_ends(partners, low, edges, mate, cross, query):
    columns, channels = query.shape[1:]
    row = jax.ShapeDtypeStruct((1, columns, channels), jnp.bfloat16)
    operands = [*edges, mate, cross, query]
    return pl.pallas_call(
        functools.partial(attend_ends_body, low, len(edges)),
        in_specs=[in_smem] + [in_vmem] * len(operands),
        out_specs=[in_vmem] * (1 + 2 * mate.shape[0]),
        out_shape=[jax.ShapeDtypeStruct((2, columns, channels), jnp.bfloat16)]
        + [row] * (2 * mate.shape[0]),
        scratch_shapes=[pltpu.VMEM((6, columns, channels), jnp.bfloat16)],
        compiler_params=pltpu.CompilerParams(vmem_limit_bytes=vmem_bytes),
        cost_estimate=no_cost,
        name="attend_ends",
    )(partners, *operands)


def attend_outer(partners, low, sides, query, ends, state, value_out, gain, inner):
    rows, columns, channels = inner.shape
    operands = [a for group in sides for a in group]
    operands += [query, ends, state, value_out, gain, inner]
    return pl.pallas_call(
        functools.partial(attend_outer_body, low, len(sides[0])),
        in_specs=[in_smem] + [in_vmem] * len(operands),
        out_specs=anywhere,
        out_shape=jax.ShapeDtypeStruct((rows + 2, columns, channels), jnp.float32),
        scratch_shapes=[
            pltpu.VMEM((6, columns, channels), jnp.bfloat16),
            pltpu.VMEM((2, columns, channels), jnp.bfloat16),
            pltpu.VMEM((2, columns, channels), jnp.float32),
            pltpu.SemaphoreType.DMA((3,)),
        ],
        compiler_params=pltpu.CompilerParams(vmem_limit_bytes=vmem_bytes),
        cost_estimate=no_cost,
        name="attend_outer",
    )(partners, *operands)


def edge_halos_body(*refs):
    edges, (mate, cross) = refs[:-2], refs[-2:]
    odd = band_place()[2]
    for i, edge in enumerate(edges):
        mate[i] = jnp.where(odd, edge[0], edge[3])
        cross[i] = jnp.where(odd, edge[3], edge[0])


def edge_halos(edges):
    rows = jax.ShapeDtypeStruct((len(edges), *edges[0].shape[1:]), jnp.bfloat16)
    return pl.pallas_call(
        edge_halos_body,
        in_specs=[in_vmem] * len(edges),
        out_specs=[in_vmem] * 2,
        out_shape=[rows, rows],
        compiler_params=pltpu.CompilerParams(vmem_limit_bytes=vmem_bytes),
        cost_estimate=no_cost,
        name="edge_halos",
    )(*edges)


def swap(cells, views, offset):
    return lax.ppermute(cells, "view", [(i, i ^ offset) for i in range(views)])


def gather_direct(cells, views):
    return {1 << i: swap(cells, views, 1 << i) for i in range((views - 1).bit_length())}


def relay(held, views, by_low):
    for offset in range(1, views):
        bit = offset & -offset if by_low else 1 << (offset.bit_length() - 1)
        if bit != offset:
            held[offset] = swap(held[offset ^ bit], views, bit)


def swap_bands(mate, cross, bands):
    mates = [(i, i ^ 1) for i in range(bands)]
    crosses = [(i, i + 1) for i in range(1, bands - 1, 2)]
    crosses = crosses + [(j, i) for i, j in crosses]
    return lax.ppermute(mate, "band", mates), lax.ppermute(cross, "band", crosses)


def per_device(
    features, tempers, partners, conv_one, conv_two, query_weight, key_weight,
    value_weight, out_weight, norm_gain, message_gain,
):
    views = lax.axis_size("view")
    bands = lax.axis_size("band")
    cells, temper, gain = features[0], tempers[0], norm_gain[None]

    mate, cross, state_one, state_middle, middle = middle_rows(cells, conv_one, conv_two, gain)
    middles = gather_direct(middle, views)
    mate, cross = swap_bands(mate, cross, bands)
    state_edge, edge = edge_rows(cells, mate, cross, conv_one, conv_two, state_one, gain)
    edges = gather_direct(edge, views)

    def candidates(groups, low, high):
        return [[group[i] for i in range(low, high + 1)] for group in groups]

    near_ends, far_ends = (1, max(1, views - 2)), (min(2, views - 1), views - 1)
    direct = list(edges)
    *queries, first = attend_first(
        partners, 1, [middles[i] for i in direct], edge, middle, query_weight, key_weight, temper
    )
    value_out = jnp.dot(value_weight, out_weight, preferred_element_type=jnp.float32).astype(
        jnp.bfloat16
    )
    edges, middles, queries, first, value_out = lax.optimization_barrier(
        (edges, middles, queries, first, value_out)
    )
    mate, cross = swap_bands(*edge_halos([edges[i] for i in direct]), bands)
    relay(edges, views, False)
    relay(middles, views, True)
    near = attend_near(partners, near_ends[0], candidates((edges, middles), *near_ends), queries)
    mate, cross, near = lax.optimization_barrier((mate, cross, near))
    near_edges = candidates((edges,), *near_ends)[0]
    ends, *halos = attend_ends(partners, near_ends[0], near_edges, mate, cross, queries[0])
    halos, ends = lax.optimization_barrier((halos, ends))
    above = dict(zip(direct, halos[0::2]))
    below = dict(zip(direct, halos[1::2]))
    relay(above, views, True)
    relay(below, views, False)
    rest = (value_out, message_gain[None])
    inner = attend_far(
        partners, far_ends[0], candidates((edges, middles), *far_ends), queries, near, first,
        (state_edge, state_middle), *rest,
    )
    refined = attend_outer(
        partners, far_ends[0], candidates((edges, above, below), *far_ends), queries[0], ends,
        state_edge, *rest, inner,
    )
    return refined[None]


def solution(mesh):
    whole = P()
    in_specs = (P("view", "band", None, None), P("view", "band", None)) + (whole,) * 9
    return jax.shard_map(
        per_device, mesh=mesh, in_specs=in_specs,
        out_specs=P("view", "band", None, None), check_vma=False,
    )
```

```python
import functools
import math

import jax
import jax.numpy as jnp
from jax import lax
from jax.experimental import pallas as pl
from jax.experimental.pallas import tpu as pltpu
from jax.sharding import PartitionSpec as P

epsilon = 1e-06
vmem_bytes = 28 * 1024 * 1024
edge_vmem_bytes = 40 * 1024 * 1024
whole_vmem_bytes = 56 * 1024 * 1024
in_vmem = pl.BlockSpec(memory_space=pltpu.VMEM)
in_smem = pl.BlockSpec(memory_space=pltpu.SMEM)
no_cost = pl.CostEstimate(flops=0, bytes_accessed=0, transcendentals=0)
anywhere = pl.BlockSpec(memory_space=pl.ANY)


def silu(v):
    half = 0.5 * v
    return half * jnp.tanh(half) + half


def scaled(values, gain):
    mean_square = jnp.mean(values * values, axis=-1, keepdims=True)
    return values * lax.rsqrt(mean_square + epsilon) * gain


class Copies:
    def __init__(self, semaphores):
        self.semaphores = semaphores
        self.count = 0

    def start(self, source, target):
        copy = pltpu.make_async_copy(source, target, self.semaphores.at[self.count])
        self.count += 1
        copy.start()
        return copy

    def start_one(self, sources, chosen, target):
        slot = self.semaphores.at[self.count]
        self.count += 1
        for i, source in enumerate(sources):

            @pl.when(chosen == i)
            def _(source=source):
                pltpu.make_async_copy(source, target, slot).start()

        return pltpu.make_async_copy(sources[0], target, slot)


def clear(pad):
    slots, length, channels = pad.shape
    zeros = jnp.zeros((8, channels), jnp.float32)
    for slot in range(slots):
        pad[slot, 0:8] = zeros
        pad[slot, length - 8 : length] = zeros


def place(value, pad, slot):
    pad[slot, 8 : 8 + value.shape[0]] = value


def pack(kernel, out):
    channels = kernel.shape[2]
    zero = jnp.zeros((channels, channels), jnp.bfloat16)
    for j in range(4):
        for b in range(3):
            rows = pl.ds((3 * j + b) * channels, channels)
            out[rows, :channels] = kernel[j, b] if j < 3 else zero
            out[rows, channels:] = kernel[j - 1, b] if j > 0 else zero


def row_pair(pad, first, weights):
    columns = pad.shape[1] - 16
    block = 128 if columns % 128 == 0 else columns
    outs = []
    for start in range(7, 7 + columns, block):
        lhs = [pad[first + j, start + b : start + b + block] for j in range(4) for b in range(3)]
        lhs = jnp.concatenate(lhs, axis=-1).astype(jnp.bfloat16)
        outs.append(jnp.dot(lhs, weights[...], preferred_element_type=jnp.float32))
    return jnp.concatenate(outs, axis=0)


def ask(norm, query_weight, key_weight, tempers, query_edge, query_middle):
    rows, channels = tempers.shape[0], norm[0].shape[-1]
    mixing = lax.dot_general(
        query_weight[...],
        key_weight[...],
        (((1,), (1,)), ((), ())),
        preferred_element_type=jnp.float32,
    ).astype(jnp.bfloat16)
    scales = tempers[...].T * (math.log2(math.e) / math.sqrt(channels))
    for r in range(rows):
        row = band_row(*norm, r)[...]
        mixed = jnp.dot(row, mixing, preferred_element_type=jnp.float32)
        query = (mixed * scales[:, r : r + 1]).astype(jnp.bfloat16)
        band_row(query_edge, query_middle, r)[...] = query


def middle_body(
    cells, one, two, gain, mate_out, cross_out, state_one_out, state_out, norm_out,
    held, one_held, two_held, gain_held, mate, cross, w1, w2, state_one, state_two, norm, x1, x2,
    sems,
):
    rows = cells.shape[0]
    channels = cells.shape[2]
    copies = Copies(sems)
    kernels = [copies.start(one, one_held), copies.start(two, two_held)]
    loads = [copies.start(cells.at[r], held.at[r]) for r in range(4)]
    later = [copies.start(cells.at[r], held.at[r]) for r in range(4, rows)]
    later.append(copies.start(gain, gain_held))
    clear(x1)
    clear(x2)

    def convolve_one(first):
        out = row_pair(x1, first, w1)
        for o in range(2):
            r = first + 1 + o
            state = held[r] + out[:, o * channels : (o + 1) * channels]
            state_one[r - 1] = state
            place(silu(state), x2, r - 1)

    def convolve_two(first):
        out = row_pair(x2, first, w2)
        for o in range(2):
            slot = first + o
            state = state_one[slot + 1] + out[:, o * channels : (o + 1) * channels]
            state_two[slot] = state
            norm[slot] = scaled(state, gain_held[...]).astype(jnp.bfloat16)

    for load in kernels:
        load.wait()
    pack(one_held, w1)
    pack(two_held, w2)
    for load in loads:
        load.wait()
    for r in range(4):
        place(silu(held[r]), x1, r)
    for load in later:
        load.wait()
    odd = band_place()[2]
    for r in range(2):
        head, tail = held[r].astype(jnp.bfloat16), held[rows - 2 + r].astype(jnp.bfloat16)
        mate[r] = jnp.where(odd, head, tail)
        cross[r] = jnp.where(odd, tail, head)
    for first in range(0, rows - 2, 2):
        convolve_one(first)
        for r in range(first + 4, min(first + 6, rows)):
            place(silu(held[r]), x1, r)
    early = [
        copies.start(mate, mate_out),
        copies.start(cross, cross_out),
        copies.start(state_one.at[pl.ds(0, 2)], state_one_out.at[pl.ds(0, 2)]),
        copies.start(state_one.at[pl.ds(rows - 4, 2)], state_one_out.at[pl.ds(2, 2)]),
    ]
    for first in range(0, rows - 6, 2):
        convolve_two(first)
    stores = early + [
        copies.start(state_two.at[pl.ds(0, rows - 6)], state_out.at[pl.ds(0, rows - 6)]),
        copies.start(norm.at[pl.ds(0, rows - 6)], norm_out.at[pl.ds(0, rows - 6)]),
    ]
    convolve_two(rows - 6)
    last = pl.ds(rows - 6, 2)
    stores += [
        copies.start(norm.at[last], norm_out.at[last]),
        copies.start(state_two.at[last], state_out.at[last]),
    ]
    for store in stores:
        store.wait()


def scratch(*arrays):
    return [pltpu.VMEM(shape, kind) for shape, kind in arrays]


def middle_rows(cells, one, two, gain):
    rows, columns, channels = cells.shape
    row = (columns, channels)
    padded = (columns + 16, channels)
    packed = ((12 * channels, 2 * channels), jnp.bfloat16)
    operands = (cells, one, two, gain)
    return pl.pallas_call(
        middle_body,
        in_specs=[anywhere] * 4,
        out_specs=[anywhere] * 5,
        out_shape=[
            jax.ShapeDtypeStruct((2, *row), jnp.bfloat16),
            jax.ShapeDtypeStruct((2, *row), jnp.bfloat16),
            jax.ShapeDtypeStruct((4, *row), jnp.float32),
            jax.ShapeDtypeStruct((rows - 4, *row), jnp.float32),
            jax.ShapeDtypeStruct((rows - 4, *row), jnp.bfloat16),
        ],
        scratch_shapes=[
            *scratch(*[(a.shape, a.dtype) for a in operands]),
            *scratch(
                ((2, *row), jnp.bfloat16),
                ((2, *row), jnp.bfloat16),
                packed,
                packed,
                ((rows - 2, *row), jnp.float32),
                ((rows - 4, *row), jnp.float32),
                ((rows - 4, *row), jnp.bfloat16),
                ((rows, *padded), jnp.float32),
                ((rows - 2, *padded), jnp.float32),
            ),
            pltpu.SemaphoreType.DMA((rows + 11,)),
        ],
        compiler_params=pltpu.CompilerParams(vmem_limit_bytes=whole_vmem_bytes),
        cost_estimate=no_cost,
        name="residual_middle",
    )(*operands)


def edge_body(
    cells, mate, cross, one, two, state_one, gain, state_out, norm_out,
    held, one_held, two_held, state_held, gain_held, w1, w2, state_two, norm, x1, x2, sems,
):
    rows = cells.shape[0]
    channels = cells.shape[2]
    first_band, last_band, odd = band_place()
    copies = Copies(sems)
    loads = [
        copies.start(cells.at[pl.ds(0, 2)], held.at[pl.ds(0, 2)]),
        copies.start(cells.at[pl.ds(rows - 2, 2)], held.at[pl.ds(2, 2)]),
    ]
    later = [
        copies.start(one, one_held),
        copies.start(two, two_held),
        copies.start(state_one, state_held),
        copies.start(gain, gain_held),
    ]
    clear(x1)
    clear(x2)
    for load in loads:
        load.wait()
    for r in range(2):
        place(silu(held[r]), x1, 2 + r)
        place(silu(held[2 + r]), x1, 4 + r)
    outside = []
    for r in range(2):
        mate_row = mate[r].astype(jnp.float32)
        cross_row = cross[r].astype(jnp.float32)
        over = jnp.where(first_band, 0.0, jnp.where(odd, mate_row, cross_row))
        under = jnp.where(last_band, 0.0, jnp.where(odd, cross_row, mate_row))
        place(silu(over), x1, r)
        place(silu(under), x1, 6 + r)
        outside.append((over, under))
    over, under = outside[1][0], outside[0][1]
    for load in later:
        load.wait()
    pack(one_held, w1)
    pack(two_held, w2)
    out = row_pair(x1, 0, w1)
    over = over + out[:, :channels]
    top = held[0] + out[:, channels:]
    out = row_pair(x1, 4, w1)
    bottom = held[3] + out[:, :channels]
    under = under + out[:, channels:]
    for r in range(2):
        place(silu(state_held[r]), x2, 2 + r)
        place(silu(state_held[2 + r]), x2, 4 + r)
    place(jnp.where(first_band, 0.0, silu(over)), x2, 0)
    place(silu(top), x2, 1)
    place(silu(bottom), x2, 6)
    place(jnp.where(last_band, 0.0, silu(under)), x2, 7)
    for slot, states in ((0, (top, state_held[0])), (2, (state_held[3], bottom))):
        out = row_pair(x2, 2 * slot, w2)
        for o in range(2):
            state = states[o] + out[:, o * channels : (o + 1) * channels]
            state_two[slot + o] = state
            norm[slot + o] = scaled(state, gain_held[...]).astype(jnp.bfloat16)
    stores = [copies.start(norm, norm_out), copies.start(state_two, state_out)]
    for store in stores:
        store.wait()


def edge_rows(cells, mate, cross, one, two, state_one, gain):
    columns, channels = cells.shape[1:]
    row = (columns, channels)
    padded = (columns + 16, channels)
    packed = ((12 * channels, 2 * channels), jnp.bfloat16)
    operands = (cells, mate, cross, one, two, state_one, gain)
    return pl.pallas_call(
        edge_body,
        in_specs=[anywhere] + [in_vmem] * 2 + [anywhere] * 4,
        out_specs=[anywhere] * 2,
        out_shape=[
            jax.ShapeDtypeStruct((4, *row), jnp.float32),
            jax.ShapeDtypeStruct((4, *row), jnp.bfloat16),
        ],
        scratch_shapes=[
            *scratch(((4, *row), jnp.float32), *[(a.shape, a.dtype) for a in operands[3:]]),
            *scratch(
                packed,
                packed,
                ((4, *row), jnp.float32),
                ((4, *row), jnp.bfloat16),
                ((8, *padded), jnp.float32),
                ((8, *padded), jnp.float32),
            ),
            pltpu.SemaphoreType.DMA((8,)),
        ],
        compiler_params=pltpu.CompilerParams(vmem_limit_bytes=edge_vmem_bytes),
        cost_estimate=no_cost,
        name="residual_edge",
    )(*operands)


def band_place():
    band = lax.axis_index("band")
    return band == 0, band == lax.axis_size("band") - 1, lax.rem(band, 2) == 1


def blend(query, window, store):
    keys, channels = window.shape
    extended = jnp.concatenate([window, jnp.ones((keys, channels), jnp.bfloat16)], axis=1)
    columns = query.shape[0]
    block = 128 if columns % 128 == 0 else columns
    for start in range(0, columns, block):
        scores = lax.dot_general(
            query[pl.ds(start, block)],
            window,
            (((1,), (1,)), ((), ())),
            preferred_element_type=jnp.float32,
        )
        peak = jnp.max(scores, axis=-1, keepdims=True)
        lifted = jnp.exp2(scores - peak).astype(jnp.bfloat16)
        total = jnp.dot(lifted, extended, preferred_element_type=jnp.float32)
        store(pl.ds(start, block), total[:, :channels] / total[:, channels:])


def pick(chosen, candidates):
    picked = candidates[0]
    for i, candidate in enumerate(candidates[1:], 1):
        picked = jnp.where(chosen == i, candidate, picked)
    return picked


def key_offset(partners, low, far):
    view = lax.axis_index("view")
    first = jnp.bitwise_xor(partners[view, 0], view)
    second = jnp.bitwise_xor(partners[view, 1], view)
    return (jnp.maximum(first, second) if far else jnp.minimum(first, second)) - low


def band_row(edge, middle, r):
    inner = middle.shape[0]
    if r < 2:
        return edge.at[r]
    if r < inner + 2:
        return middle.at[r - 2]
    return edge.at[r - inner]


def picked_row(chosen, edges, middles, r):
    return pick(chosen, [band_row(e, m, r)[...] for e, m in zip(edges, middles)])


def finish(r, both, state, value_out, gain, result):
    message = jnp.dot(both[r], value_out[...], preferred_element_type=jnp.float32)
    result[r] = state[...] + scaled(message, gain[...])


def take(refs, *counts):
    groups = []
    for count in counts:
        groups.append(refs[:count])
        refs = refs[count:]
    return (*groups, refs)


def gather_keys(chosen, edges, middles, keys):
    for r in range(keys.shape[0]):
        keys[r] = pick(chosen, [band_row(e, m, r)[...] for e, m in zip(edges, middles)])


def attend_first_body(low, count, partners, *refs):
    middles, refs = take(refs, count)
    (
        edge, middle, query_weight, key_weight, tempers, query_edge, query_middle, out, keys
    ) = refs
    ask((edge, middle), query_weight, key_weight, tempers, query_edge, query_middle)
    columns, channels = out.shape[1:]
    chosen = key_offset(partners, low, False)
    for r in range(keys.shape[0]):
        keys[r] = pick(chosen, [m[r] for m in middles])
    for r in range(out.shape[0]):
        window = keys[r : r + 3].reshape(3 * columns, channels)

        def store(place, value, r=r):
            out[r, place] = value.astype(jnp.bfloat16)

        blend(query_middle.at[r + 1], window, store)


def attend_near_body(low, count, partners, *refs):
    edges, middles, refs = take(refs, count, count)
    query_edge, query_middle, out, keys = refs
    rows, columns, channels = keys.shape
    gather_keys(key_offset(partners, low, False), edges, middles, keys)
    for slot, r in enumerate((1, 2, rows - 3, rows - 2)):
        window = keys[r - 1 : r + 2].reshape(3 * columns, channels)

        def store(place, value, slot=slot):
            out[slot, place] = value.astype(jnp.bfloat16)

        blend(band_row(query_edge, query_middle, r), window, store)


def attend_far_body(low, count, partners, *refs):
    edges, middles, refs = take(refs, count, count)
    (
        query_edge, query_middle, near, first, state_edge, state_middle, value_out, gain,
        out, keys, both,
    ) = refs
    rows, columns, channels = keys.shape
    gather_keys(key_offset(partners, low, True), edges, middles, keys)
    for r in range(1, rows - 1):
        window = keys[r - 1 : r + 2].reshape(3 * columns, channels)
        other = band_row(near, first, r - 1)

        def store(place, value, r=r, other=other):
            both[r - 1, place] = (value + other[place].astype(jnp.float32)).astype(jnp.bfloat16)

        blend(band_row(query_edge, query_middle, r), window, store)
    for r in range(1, rows - 1):
        finish(r - 1, both, band_row(state_edge, state_middle, r), value_out, gain, out)


def end_windows(chosen, edges, above, below, keys):
    keys[0] = above
    keys[5] = below
    for r in range(4):
        keys[1 + r] = pick(chosen, [e[r] for e in edges])


def attend_ends_body(low, count, partners, *refs):
    edges, refs = take(refs, count)
    mate, cross, query_edge, out = refs[:4]
    outs, keys = refs[4:-1], refs[-1]
    columns, channels = out.shape[1:]
    first_band, last_band, odd = band_place()
    for i in range(mate.shape[0]):
        above = jnp.where(odd, mate[i], cross[i])
        below = jnp.where(odd, cross[i], mate[i])
        outs[2 * i][0] = jnp.where(first_band, jnp.zeros_like(above), above)
        outs[2 * i + 1][0] = jnp.where(last_band, jnp.zeros_like(below), below)
    chosen = key_offset(partners, low, False)
    above = pick(chosen, [a[0] for a in outs[0::2]])
    below = pick(chosen, [b[0] for b in outs[1::2]])
    end_windows(chosen, edges, above, below, keys)
    for end in range(2):
        window = keys[3 * end : 3 * end + 3].reshape(3 * columns, channels)

        def store(place, value, end=end):
            out[end, place] = value.astype(jnp.bfloat16)

        blend(query_edge.at[3 * end], window, store)


def attend_outer_body(low, count, partners, *refs):
    edges, aboves, belows, refs = take(refs, count, count, count)
    query_edge, ends, state_edge, value_out, gain, inner, out, keys, both, result, sems = refs
    rows, columns, channels = out.shape
    copies = Copies(sems)
    stores = [copies.start(inner, out.at[pl.ds(1, rows - 2)])]
    chosen = key_offset(partners, low, True)
    above = pick(chosen, [a[0] for a in aboves])
    below = pick(chosen, [b[0] for b in belows])
    end_windows(chosen, edges, above, below, keys)
    for end in range(2):
        window = keys[3 * end : 3 * end + 3].reshape(3 * columns, channels)

        def store(place, value, end=end):
            both[end, place] = (value + ends[end, place].astype(jnp.float32)).astype(jnp.bfloat16)

        blend(query_edge.at[3 * end], window, store)
    for end in range(2):
        finish(end, both, state_edge.at[3 * end], value_out, gain, result)
    stores += [copies.start(result.at[0], out.at[0]), copies.start(result.at[1], out.at[rows - 1])]
    for store in stores:
        store.wait()


def attend_first(partners, low, middles, edge, middle, query_weight, key_weight, tempers):
    rows, columns = tempers.shape
    channels = edge.shape[-1]
    operands = [*middles, edge, middle, query_weight, key_weight, tempers]
    like = jax.ShapeDtypeStruct
    return pl.pallas_call(
        functools.partial(attend_first_body, low, len(middles)),
        in_specs=[in_smem] + [in_vmem] * len(operands),
        out_specs=[in_vmem] * 3,
        out_shape=[
            like(edge.shape, jnp.bfloat16),
            like(middle.shape, jnp.bfloat16),
            like((rows - 6, columns, channels), jnp.bfloat16),
        ],
        scratch_shapes=[pltpu.VMEM(middle.shape, jnp.bfloat16)],
        compiler_params=pltpu.CompilerParams(vmem_limit_bytes=vmem_bytes),
        cost_estimate=no_cost,
        name="attend_first",
    )(partners, *operands)


def attend_near(partners, low, candidates, queries):
    rows = candidates[0][0].shape[0] + candidates[1][0].shape[0]
    columns, channels = queries[0].shape[1:]
    operands = [a for group in candidates for a in group] + list(queries)
    return pl.pallas_call(
        functools.partial(attend_near_body, low, len(candidates[0])),
        in_specs=[in_smem] + [in_vmem] * len(operands),
        out_specs=in_vmem,
        out_shape=jax.ShapeDtypeStruct((4, columns, channels), jnp.bfloat16),
        scratch_shapes=[pltpu.VMEM((rows, columns, channels), jnp.bfloat16)],
        compiler_params=pltpu.CompilerParams(vmem_limit_bytes=vmem_bytes),
        cost_estimate=no_cost,
        name="attend_near",
    )(partners, *operands)


def attend_far(partners, low, candidates, queries, near, first, states, value_out, gain):
    columns, channels = near.shape[1:]
    rows = near.shape[0] + first.shape[0]
    operands = [a for group in candidates for a in group]
    operands += [*queries, near, first, *states, value_out, gain]
    return pl.pallas_call(
        functools.partial(attend_far_body, low, len(candidates[0])),
        in_specs=[in_smem] + [in_vmem] * len(operands),
        out_specs=in_vmem,
        out_shape=jax.ShapeDtypeStruct((rows, columns, channels), jnp.float32),
        scratch_shapes=[
            pltpu.VMEM((rows + 2, columns, channels), jnp.bfloat16),
            pltpu.VMEM((rows, columns, channels), jnp.bfloat16),
        ],
        compiler_params=pltpu.CompilerParams(vmem_limit_bytes=vmem_bytes),
        cost_estimate=no_cost,
        name="attend_far",
    )(partners, *operands)


def attend_ends(partners, low, edges, mate, cross, query):
    columns, channels = query.shape[1:]
    row = jax.ShapeDtypeStruct((1, columns, channels), jnp.bfloat16)
    operands = [*edges, mate, cross, query]
    return pl.pallas_call(
        functools.partial(attend_ends_body, low, len(edges)),
        in_specs=[in_smem] + [in_vmem] * len(operands),
        out_specs=[in_vmem] * (1 + 2 * mate.shape[0]),
        out_shape=[jax.ShapeDtypeStruct((2, columns, channels), jnp.bfloat16)]
        + [row] * (2 * mate.shape[0]),
        scratch_shapes=[pltpu.VMEM((6, columns, channels), jnp.bfloat16)],
        compiler_params=pltpu.CompilerParams(vmem_limit_bytes=vmem_bytes),
        cost_estimate=no_cost,
        name="attend_ends",
    )(partners, *operands)


def attend_outer(partners, low, sides, query, ends, state, value_out, gain, inner):
    rows, columns, channels = inner.shape
    operands = [a for group in sides for a in group]
    operands += [query, ends, state, value_out, gain, inner]
    return pl.pallas_call(
        functools.partial(attend_outer_body, low, len(sides[0])),
        in_specs=[in_smem] + [in_vmem] * len(operands),
        out_specs=anywhere,
        out_shape=jax.ShapeDtypeStruct((rows + 2, columns, channels), jnp.float32),
        scratch_shapes=[
            pltpu.VMEM((6, columns, channels), jnp.bfloat16),
            pltpu.VMEM((2, columns, channels), jnp.bfloat16),
            pltpu.VMEM((2, columns, channels), jnp.float32),
            pltpu.SemaphoreType.DMA((3,)),
        ],
        compiler_params=pltpu.CompilerParams(vmem_limit_bytes=vmem_bytes),
        cost_estimate=no_cost,
        name="attend_outer",
    )(partners, *operands)


def edge_halos_body(*refs):
    edges, (mate, cross) = refs[:-2], refs[-2:]
    odd = band_place()[2]
    for i, edge in enumerate(edges):
        mate[i] = jnp.where(odd, edge[0], edge[3])
        cross[i] = jnp.where(odd, edge[3], edge[0])


def edge_halos(edges):
    rows = jax.ShapeDtypeStruct((len(edges), *edges[0].shape[1:]), jnp.bfloat16)
    return pl.pallas_call(
        edge_halos_body,
        in_specs=[in_vmem] * len(edges),
        out_specs=[in_vmem] * 2,
        out_shape=[rows, rows],
        compiler_params=pltpu.CompilerParams(vmem_limit_bytes=vmem_bytes),
        cost_estimate=no_cost,
        name="edge_halos",
    )(*edges)


def swap(cells, views, offset):
    return lax.ppermute(cells, "view", [(i, i ^ offset) for i in range(views)])


def gather_direct(cells, views):
    return {1 << i: swap(cells, views, 1 << i) for i in range((views - 1).bit_length())}


def relay(held, views, by_low):
    for offset in range(1, views):
        bit = offset & -offset if by_low else 1 << (offset.bit_length() - 1)
        if bit != offset:
            held[offset] = swap(held[offset ^ bit], views, bit)


def swap_bands(mate, cross, bands):
    mates = [(i, i ^ 1) for i in range(bands)]
    crosses = [(i, i + 1) for i in range(1, bands - 1, 2)]
    crosses = crosses + [(j, i) for i, j in crosses]
    return lax.ppermute(mate, "band", mates), lax.ppermute(cross, "band", crosses)


def per_device(
    features, tempers, partners, conv_one, conv_two, query_weight, key_weight,
    value_weight, out_weight, norm_gain, message_gain,
):
    views = lax.axis_size("view")
    bands = lax.axis_size("band")
    cells, temper, gain = features[0], tempers[0], norm_gain[None]

    mate, cross, state_one, state_middle, middle = middle_rows(cells, conv_one, conv_two, gain)
    middles = gather_direct(middle, views)
    mate, cross = swap_bands(mate, cross, bands)
    state_edge, edge = edge_rows(cells, mate, cross, conv_one, conv_two, state_one, gain)
    edges = gather_direct(edge, views)

    def candidates(groups, low, high):
        return [[group[i] for i in range(low, high + 1)] for group in groups]

    near_ends, far_ends = (1, max(1, views - 2)), (min(2, views - 1), views - 1)
    direct = list(edges)
    *queries, first = attend_first(
        partners, 1, [middles[i] for i in direct], edge, middle, query_weight, key_weight, temper
    )
    value_out = jnp.dot(value_weight, out_weight, preferred_element_type=jnp.float32).astype(
        jnp.bfloat16
    )
    edges, middles, queries, first, value_out = lax.optimization_barrier(
        (edges, middles, queries, first, value_out)
    )
    mate, cross = swap_bands(*edge_halos([edges[i] for i in direct]), bands)
    relay(edges, views, False)
    relay(middles, views, True)
    near = attend_near(partners, near_ends[0], candidates((edges, middles), *near_ends), queries)
    mate, cross, near = lax.optimization_barrier((mate, cross, near))
    near_edges = candidates((edges,), *near_ends)[0]
    ends, *halos = attend_ends(partners, near_ends[0], near_edges, mate, cross, queries[0])
    edges, middles, halos, ends = lax.optimization_barrier((edges, middles, halos, ends))
    above = dict(zip(direct, halos[0::2]))
    below = dict(zip(direct, halos[1::2]))
    relay(above, views, True)
    relay(below, views, False)
    rest = (value_out, message_gain[None])
    inner = attend_far(
        partners, far_ends[0], candidates((edges, middles), *far_ends), queries, near, first,
        (state_edge, state_middle), *rest,
    )
    refined = attend_outer(
        partners, far_ends[0], candidates((edges, above, below), *far_ends), queries[0], ends,
        state_edge, *rest, inner,
    )
    return refined[None]


def solution(mesh):
    whole = P()
    in_specs = (P("view", "band", None, None), P("view", "band", None)) + (whole,) * 9
    return jax.shard_map(
        per_device, mesh=mesh, in_specs=in_specs,
        out_specs=P("view", "band", None, None), check_vma=False,
    )
```
